512 devices in a mesh: wide: 128 (over z_lo, y, x), narrow: 4 (over z_hi, core).
Axes of the slice: x: 4, y: 8, z: 8 (z_hi: 2, z_lo: 4; z = z_hi * 4 + z_lo), core: 2. Of those that a mesh axis runs over, the one named last changes fastest.
Arguments:
- adjoint_velocity: float32 [3, 2048, 128, 128], P(None, 'wide', 'narrow'), may hold values from -60 to 60
- coefficient: float32 [2048, 128, 128], P('wide', 'narrow'), may hold values from 0.5 to 2
- record_counts: int32 [128, 4], P('wide', 'narrow'), may hold values from 256 to 1024, as said below
- record_cells: int32 [128, 4, 3, 1024], P('wide', 'narrow'), may hold values from 0 to 127, as said below
- record_offsets: float32 [128, 4, 3, 1024], P('wide', 'narrow'), may hold values from 0 to 1
Outputs:
- smoothed: float32 [3, 2048, 128, 128], P(None, 'wide', 'narrow')
- moment_grad: float32 [128, 4, 12, 1024], P('wide', 'narrow')
The draws below stay inside these ranges and needn't reach their ends.
Inputs may be any that keep to these rules, and one draw needn't show every extreme that they name: Slots 0 to record_counts - 1 of a tile hold live records, the others padding; in every draw some tile has all 1024 slots live. `record_cells`: component 0 lies in 0 to 15, component 1 in 0 to 31, component 2 in 0 to 127. Of a tile's 1024 slots, exactly 256 have component 0 below 4 and exactly 256 have it at 12 or above; exactly 128 have component 1 below 4 and exactly 128 have it at 28 or above; each of the four pairings of a low or high component 0 with a low or high component 1 holds exactly 32 slots.
All inputs are finite; a program needn't handle non-finite values.
Results may differ from the reference program's by a relative error of at most 0.0003.
Values sent between devices are 32-bit elements; how exact they have to be, the bound alone decides.
A program may use at most 64 MiB of HBM per device.

```python
import math
import jax
import jax.numpy as jnp
from jax import lax

CX = 16
CY = 32
NZ = 128
SLOTS = 1024
RADIUS = 4
SWEEPS = 4
EDGE_X = 256
EDGE_Y = 128
CORNER = 32
TILES_X = 128
TILES_Y = 4
NX = 2048
NY = 128


def draw_record_counts(key, part):
    tiles = TILES_X * TILES_Y
    counts = jax.random.randint(jax.random.fold_in(key, 11), (tiles,), SLOTS // 4, 3 * SLOTS // 4 + 1)
    full_tile = jax.random.randint(jax.random.fold_in(key, 12), (), 0, tiles)
    counts = counts.at[full_tile].set(SLOTS)
    return counts.reshape(TILES_X, TILES_Y).astype(jnp.int32)


def draw_record_cells(key, part):
    tiles = TILES_X * TILES_Y
    keys = jax.random.split(jax.random.fold_in(key, 20), tiles)
    ranks = jax.vmap(lambda one: jax.random.permutation(one, SLOTS))(keys).reshape(TILES_X, TILES_Y, SLOTS)
    edge_x = EDGE_X
    edge_y = EDGE_Y
    corner = CORNER
    bound_a = corner
    bound_b = 2 * corner
    bound_c = 3 * corner
    bound_d = 4 * corner
    bound_e = bound_d + edge_x - 2 * corner
    bound_f = bound_e + edge_x - 2 * corner
    bound_g = bound_f + edge_y - 2 * corner
    bound_h = bound_g + edge_y - 2 * corner
    tests = [ranks < bound_a, ranks < bound_b, ranks < bound_c, ranks < bound_d, ranks < bound_e, ranks < bound_f, ranks < bound_g, ranks < bound_h]
    class_x = jnp.select(tests, [0, 0, 1, 1, 0, 1, 2, 2], 2)
    class_y = jnp.select(tests, [0, 1, 0, 1, 2, 2, 0, 1], 2)
    shape = (TILES_X, TILES_Y, SLOTS)
    low_x = jax.random.randint(jax.random.fold_in(key, 21), shape, 0, RADIUS)
    high_x = jax.random.randint(jax.random.fold_in(key, 22), shape, CX - RADIUS, CX)
    middle_x = jax.random.randint(jax.random.fold_in(key, 23), shape, RADIUS, CX - RADIUS)
    low_y = jax.random.randint(jax.random.fold_in(key, 24), shape, 0, RADIUS)
    high_y = jax.random.randint(jax.random.fold_in(key, 25), shape, CY - RADIUS, CY)
    middle_y = jax.random.randint(jax.random.fold_in(key, 26), shape, RADIUS, CY - RADIUS)
    first = jnp.where(class_x == 0, low_x, jnp.where(class_x == 1, high_x, middle_x))
    second = jnp.where(class_y == 0, low_y, jnp.where(class_y == 1, high_y, middle_y))
    third = jax.random.randint(jax.random.fold_in(key, 27), shape, 0, NZ)
    return jnp.stack([first, second, third], axis=2).astype(jnp.int32)


def shard_levels(own_key, extent, shards, least, high):
    factor_of, own = 1.0, jax.random.fold_in(own_key, 6)
    for axis_at, blocks in shards:
        heights = jnp.exp(jax.random.uniform(jax.random.fold_in(own, axis_at), (blocks,), jnp.float32, least / len(shards), high / len(shards)))
        factor_of = factor_of * jnp.repeat(heights, extent[axis_at] // blocks).reshape([-1 if axis == axis_at else 1 for axis in range(len(extent))])
    return factor_of


def gaussian(stream_key, dims, scale, most, shards=(), kind=jnp.bfloat16):
    factor_of = shard_levels(stream_key, dims, shards, -0.22, 0.18) if shards else 1.0
    drawn = jax.random.normal(stream_key, dims, jnp.float32) * scale * factor_of
    return jnp.minimum(jnp.maximum(drawn, -most), most).astype(kind)


def setup_inputs(seed: int = 0) -> dict:
    streams_of = jax.random.split(jax.random.key(seed), 6)
    return {
        "adjoint_velocity": gaussian(streams_of[0], (3, NX, NY, NZ), 10.0, 60.0, ((1, 128), (2, 4)), jnp.float32),
        "coefficient": jnp.clip(jnp.exp(math.log(2.0) - 1.3862944 * jax.random.uniform(streams_of[1], (NX, NY, NZ), jnp.float32) ** shard_levels(streams_of[1], (NX, NY, NZ), ((0, 128), (1, 4)), -0.2, 0.2)), 0.5, 2.0),
        "record_counts": draw_record_counts(jax.random.fold_in(streams_of[5], 71), 0),
        "record_cells": draw_record_cells(jax.random.fold_in(streams_of[5], 71), 0),
        "record_offsets": jnp.clip(1.0 * jax.random.uniform(streams_of[4], (TILES_X, TILES_Y, 3, SLOTS), jnp.float32) ** shard_levels(streams_of[4], (TILES_X, TILES_Y, 3, SLOTS), ((0, 128), (1, 4)), -0.2, 0.2), 0.0, 1.0),
    }


envelope_width = 1.25
relax_factor = 0.8
diag_shift = 1.0

def profile(distance):
    width_sq = envelope_width * envelope_width
    base = jnp.exp(-distance * distance / (2.0 * width_sq)) / (envelope_width * math.sqrt(2.0 * math.pi))
    first = -distance / width_sq * base
    second = (distance * distance / width_sq - 1.0) / width_sq * base
    return (base, first, second)

def neighbour_views(padded):
    return [padded[..., 2:, 1:-1, 1:-1], padded[..., :-2, 1:-1, 1:-1], padded[..., 1:-1, 2:, 1:-1], padded[..., 1:-1, :-2, 1:-1], padded[..., 1:-1, 1:-1, 2:], padded[..., 1:-1, 1:-1, :-2]]

def droplet_moments(window, cell, offset, live):
    highest = lax.Precision.HIGHEST
    span = jnp.arange(2 * RADIUS + 1, dtype=jnp.float32) - RADIUS
    wx0, wx1, wx2 = profile(span + 0.5 - offset[0])
    wy0, wy1, wy2 = profile(span + 0.5 - offset[1])
    places = jnp.arange(NZ, dtype=jnp.float32)
    centre_z = cell[2].astype(jnp.float32)
    inside = jnp.abs(places - centre_z) <= RADIUS
    wz = jnp.stack(profile(places + 0.5 - centre_z - offset[2]), axis=1)
    wz = jnp.where(inside[:, None], wz, jnp.zeros_like(wz))
    zed = jnp.einsum('ixyz,zk->ixyk', window, wz, precision=highest)
    along = jnp.einsum('ixyk,y->ixk', zed, wy0, precision=highest)
    slope = jnp.einsum('ixy,y->ix', zed[..., 0], wy1, precision=highest)
    bend = jnp.einsum('ixy,y->ix', zed[..., 0], wy2, precision=highest)
    dip_x = jnp.einsum('ix,x->i', along[:, :, 0], wx1, precision=highest)
    dip_y = jnp.einsum('ix,x->i', slope, wx0, precision=highest)
    dip_z = jnp.einsum('ix,x->i', along[:, :, 1], wx0, precision=highest)
    quad = jnp.einsum('ix,x->i', along[:, :, 0], wx2, precision=highest) + jnp.einsum('ix,x->i', bend + along[:, :, 2], wx0, precision=highest)
    return live * jnp.stack([dip_x, dip_y, dip_z, quad], axis=1).reshape(12)

def reference(adjoint_velocity, coefficient, record_counts, record_cells, record_offsets):
    coef_padded = jnp.pad(coefficient, 1)
    faces = [0.5 * (coefficient + view) for view in neighbour_views(coef_padded)]
    total = diag_shift + sum(faces)

    def relax_one(component):
        field = relax_factor * component / total
        for sweep in range(SWEEPS - 1):
            padded = jnp.pad(field, 1)
            beside_all = sum((face * view for face, view in zip(faces, neighbour_views(padded))))
            field = field + relax_factor * (component - total * field + beside_all) / total
        return field
    smoothed = lax.map(relax_one, adjoint_velocity)
    field_padded = jnp.pad(smoothed, ((0, 0), (RADIUS, RADIUS), (RADIUS, RADIUS), (0, 0)))
    tiles = TILES_X * TILES_Y
    tile_ids = jnp.arange(tiles, dtype=jnp.int32)
    cells_flat = record_cells.reshape(tiles, 3, SLOTS)
    offsets_flat = record_offsets.reshape(tiles, 3, SLOTS)
    counts_flat = record_counts.reshape(tiles)
    zero_index = jnp.zeros((), jnp.int32)

    def one_tile(inputs):
        tile, cells, offsets, count = inputs
        anchor_x = (tile // TILES_Y * CX).astype(jnp.int32)
        anchor_y = (tile % TILES_Y * CY).astype(jnp.int32)
        alive = (jnp.arange(SLOTS, dtype=jnp.int32) < count).astype(jnp.float32)

        def one_droplet(cell, offset, live):
            window = lax.dynamic_slice(field_padded, (zero_index, (anchor_x + cell[0]).astype(jnp.int32), (anchor_y + cell[1]).astype(jnp.int32), zero_index), (3, 2 * RADIUS + 1, 2 * RADIUS + 1, NZ))
            return droplet_moments(window, cell, offset, live)
        return jax.vmap(one_droplet, in_axes=(1, 1, 0), out_axes=1)(cells, offsets, alive)
    grads = lax.map(one_tile, (tile_ids, cells_flat, offsets_flat, counts_flat))
    return (smoothed, grads.reshape(TILES_X, TILES_Y, 12, SLOTS))
```

```python
import functools
import math

import jax
import jax.numpy as jnp
from jax import lax
from jax.experimental import pallas as pl
from jax.experimental.pallas import tpu as pltpu
from jax.sharding import PartitionSpec as P

MESH = pl.DeviceIdType.MESH
F32 = jnp.float32
BF16 = jnp.bfloat16

RADIUS = 4
CX, CY, NZ = 16, 32, 128
SLOTS = 1024
BLOCKS = SLOTS // 128
HU = 3
HC = 4
XU = CX + 2 * HU
XC = CX + 2 * HC
XW = CX + 2 * RADIUS
YA = 8
YN = CY + 8
Y0 = YA + 4
YB = YN + 16
TILES = YN // 8
KZ = 3 * NZ

WIDTH = 1.25
RELAX = 0.8

DIRS = [(dx, dy) for dx in (-1, 0, 1) for dy in (-1, 0, 1) if (dx, dy) != (0, 0)]


def profile(distance):
    width_sq = WIDTH * WIDTH
    base = jnp.exp(-distance * distance / (2.0 * width_sq)) / (WIDTH * math.sqrt(2.0 * math.pi))
    first = -distance / width_sq * base
    second = (distance * distance / width_sq - 1.0) / width_sq * base
    return (base, first, second)


def weights(places, centre, offset):
    distance = places - centre
    inside = jnp.abs(distance) <= RADIUS
    return [jnp.where(inside, item, 0.0) for item in profile(distance + 0.5 - offset)]


def split(value):
    high = value.astype(BF16)
    return high, (value - high.astype(F32)).astype(BF16)


def along(d, low, own, high):
    return (low, own, high)[d + 1]


def kernel(
    nw, nn, u_ref, k_ref, count_ref, cell_ref, off_ref, out_ref, grad_ref,
    ub, cb, w1, wa, wb, ck, xh, yh, fm, fx, fy, wz, wy, wx,
    own_sem, send_sem, recv_sem, cross_sem,
):
    a, b = lax.axis_index("wide"), lax.axis_index("narrow")
    half = nn // 2

    def exists(d):
        return (a + d[0] >= 0) & (a + d[0] < nw) & (b + d[1] >= 0) & (b + d[1] < nn)

    def same(d):
        if d[1] == 0:
            return exists(d)
        return exists(d) & ((b < half) == (b + d[1] < half))

    def cross(d):
        if d[1] == 0:
            return None
        return exists(d) & ((b < half) != (b + d[1] < half))

    def each(test, action):
        for i, d in enumerate(DIRS):
            ok = test(d)
            if ok is not None:
                pl.when(ok)(functools.partial(action, i, d))

    def number(test):
        return sum(jnp.where(test(d), 1, 0) for d in DIRS if test(d) is not None)

    def copy_of(k, i, d):
        x, y = d
        to = (a + x, b + y)

        def remote(k, src, dst):
            return pltpu.make_async_remote_copy(
                src_ref=src, dst_ref=dst, send_sem=send_sem.at[k, i], recv_sem=recv_sem.at[k, i],
                device_id=to, device_id_type=MESH,
            )

        def parts(n, lo_x, lo_y):
            src = (
                along(x, pl.ds(0, n), pl.ds(0, CX), pl.ds(CX - n, n)),
                along(y, pl.ds(0, n), pl.ds(0, CY), pl.ds(CY - n, n)),
            )
            dst = (
                along(x, pl.ds(lo_x + CX, n), pl.ds(lo_x, CX), pl.ds(lo_x - n, n)),
                along(y, pl.ds(lo_y + CY, n), pl.ds(lo_y, CY), pl.ds(lo_y - n, n)),
            )
            return src, dst

        if k == 0:
            src, dst = parts(HC, HC, Y0)
            return remote(k, k_ref.at[src], cb.at[dst])
        if k == 1:
            src, dst = parts(HU, HU, Y0)
            return remote(k, u_ref.at[:, src[0], src[1]], ub.at[:, dst[0], dst[1]])
        src, _ = parts(RADIUS, RADIUS, RADIUS)
        if x == 0:
            target = yh.at[:, :, along(y, pl.ds(4, 4), None, pl.ds(0, 4))]
        else:
            rows = along(y, pl.ds(CY + 4, 4), pl.ds(4, CY), pl.ds(0, 4))
            target = xh.at[:, along(x, pl.ds(4, 4), None, pl.ds(0, 4)), rows]
        return remote(k, out_ref.at[:, src[0], src[1]], target)

    barrier = pltpu.get_barrier_semaphore()

    def signal(semaphore):
        def action(i, d):
            pl.semaphore_signal(semaphore, inc=1, device_id=(a + d[0], b + d[1]), device_id_type=MESH)

        return action

    def send(i, d):
        for k in range(2):
            copy_of(k, i, d).start()

    each(same, signal(barrier))

    @pl.when(b < half)
    def _():
        each(cross, signal(barrier))

    own_k = pltpu.make_async_copy(k_ref, cb.at[pl.ds(HC, CX), pl.ds(Y0, CY)], own_sem.at[0])
    own_u = pltpu.make_async_copy(u_ref, ub.at[:, pl.ds(HU, CX), pl.ds(Y0, CY)], own_sem.at[1])
    own_k.start()
    own_u.start()

    @pl.when(a == 0)
    def _():
        ub[:, 0:HU] = jnp.zeros((3, HU, YB, NZ), F32)
        cb[0:HC] = jnp.zeros((HC, YB, NZ), F32)
        xh[:, 0:4] = jnp.zeros((3, 4, YN, NZ), F32)

    @pl.when(a == nw - 1)
    def _():
        ub[:, HU + CX :] = jnp.zeros((3, HU, YB, NZ), F32)
        cb[HC + CX :] = jnp.zeros((HC, YB, NZ), F32)
        xh[:, 4:8] = jnp.zeros((3, 4, YN, NZ), F32)

    @pl.when(b == 0)
    def _():
        ub[:, :, Y0 - 4 : Y0] = jnp.zeros((3, XU, 4, NZ), F32)
        cb[:, Y0 - 4 : Y0] = jnp.zeros((XC, 4, NZ), F32)
        xh[:, :, 0:4] = jnp.zeros((3, 8, 4, NZ), F32)
        yh[:, :, 0:4] = jnp.zeros((3, CX, 4, NZ), F32)

    @pl.when(b == nn - 1)
    def _():
        ub[:, :, Y0 + CY : Y0 + CY + 4] = jnp.zeros((3, XU, 4, NZ), F32)
        cb[:, Y0 + CY : Y0 + CY + 4] = jnp.zeros((XC, 4, NZ), F32)
        xh[:, :, CY + 4 :] = jnp.zeros((3, 8, 4, NZ), F32)
        yh[:, :, 4:8] = jnp.zeros((3, CX, 4, NZ), F32)

    @pl.when(b < half)
    def _():
        pl.semaphore_wait(barrier, number(same))
        each(same, send)

    @pl.when(b >= half)
    def _():
        pl.semaphore_wait(barrier, number(exists))
        each(cross, signal(cross_sem))
        each(cross, send)
        each(same, send)

    slot = lax.broadcasted_iota(jnp.int32, (1, 128), 1)

    def prepare(blk, carry):
        centre = [cell_ref[pl.ds(d * BLOCKS + blk, 1)].astype(F32) for d in range(3)]
        offset = [off_ref[pl.ds(d * BLOCKS + blk, 1)] for d in range(3)]
        live = jnp.where(slot + blk * 128 < count_ref[0, 0], 1.0, 0.0)
        rows = lax.broadcasted_iota(jnp.int32, (NZ, 128), 0).astype(F32)
        for i, item in enumerate(weights(rows, centre[2], offset[2])):
            high, low = split(item)
            wz[blk, 0:128, i * 128 : i * 128 + 128] = high
            wz[blk, 128:256, i * 128 : i * 128 + 128] = high
            wz[blk, 256:384, i * 128 : i * 128 + 128] = low
        rows = lax.broadcasted_iota(jnp.int32, (CY + YN + 8, 128), 0)
        tail = rows - CY - YN
        rows = jnp.where(rows < CY, rows, jnp.where(tail < 0, rows - CY - 4, jnp.where(tail < 4, tail - 4, tail + CY - 4)))
        for i, item in enumerate(weights(rows.astype(F32), centre[1], offset[1])):
            wy[blk, i] = item
        rows = lax.broadcasted_iota(jnp.int32, (XW, 128), 0).astype(F32) - RADIUS
        for i, item in enumerate(weights(rows, centre[0], offset[0])):
            wx[blk, i] = item * live
        return carry

    lax.fori_loop(0, BLOCKS, prepare, 0)

    @pl.when(b < half)
    def _():
        @pl.when(b == half - 1)
        def _():
            pl.semaphore_wait(cross_sem, number(cross))

        each(cross, send)

    own_k.wait()
    own_u.wait()

    def arrived(kinds):
        def action(i, d):
            j = DIRS.index((-d[0], -d[1]))
            for k in kinds:
                copy_of(k, j, DIRS[j]).wait_recv()

        return action

    each(exists, arrived((0, 1)))

    lane = lax.broadcasted_iota(jnp.int32, (8, NZ), 1)
    last_z, first_z = lane == NZ - 1, lane == 0
    y_at = lax.broadcasted_iota(jnp.int32, (8, NZ), 0) + (b * CY - 4)

    def face_coefficients(x, carry):
        x_at = a * CX - HU + x
        x_in = (x_at >= 0) & (x_at < nw * CX)
        for t in range(TILES):
            r = YA + 8 * t
            mid = cb[x + 1, r : r + 8]
            beside = [
                cb[x + 2, r : r + 8],
                cb[x, r : r + 8],
                cb[x + 1, r + 1 : r + 9],
                cb[x + 1, r - 1 : r + 7],
                jnp.where(last_z, 0.0, pltpu.roll(mid, NZ - 1, 1)),
                jnp.where(first_z, 0.0, pltpu.roll(mid, 1, 1)),
            ]
            faces = [0.5 * (mid + item) for item in beside]
            total = 1.0 + sum(faces)
            y = y_at + 8 * t
            scale = jnp.where((y >= 0) & (y < nn * CY) & x_in, RELAX / total, 0.0)
            faces[4] = jnp.where(last_z, 0.0, faces[4])
            faces[5] = jnp.where(first_z, 0.0, faces[5])
            for i, face in enumerate(faces):
                ck[i, x, 8 * t : 8 * t + 8] = scale * face
            for c in range(3):
                w1[c, x, r : r + 8] = scale * ub[c, x, r : r + 8]
        return carry

    lax.fori_loop(0, XU, face_coefficients, 0, unroll=2)

    def relaxed(src, x):
        values = [[], [], []]
        for t in range(TILES):
            r = YA + 8 * t
            k = [ck[i, x, 8 * t : 8 * t + 8] for i in range(6)]
            for c in range(3):
                mid = src[c, x, r : r + 8]
                total = (1.0 - RELAX) * mid + w1[c, x, r : r + 8]
                ends = k[4] * pltpu.roll(mid, NZ - 1, 1) + k[5] * pltpu.roll(mid, 1, 1)
                sides = k[2] * src[c, x, r + 1 : r + 9] + k[3] * src[c, x, r - 1 : r + 7]
                total += k[0] * src[c, x + 1, r : r + 8] + k[1] * src[c, x - 1, r : r + 8]
                values[c].append(total + sides + ends)
        return values

    def sweep(src, dst):
        def step(x, carry):
            values = relaxed(src, x)
            for c in range(3):
                for t in range(TILES):
                    dst[c, x, YA + 8 * t : YA + 8 * t + 8] = values[c][t]
            return carry

        return step

    lax.fori_loop(1, XU - 1, sweep(w1, wa), 0, unroll=2)
    lax.fori_loop(2, XU - 2, sweep(wa, wb), 0, unroll=2)

    def store_split(ref, index, value):
        high, low = split(value)
        ref[(*index, slice(0, 128))] = high
        ref[(*index, slice(128, 256))] = low
        ref[(*index, slice(256, 384))] = high

    def last(x, carry):
        values = relaxed(wb, x)
        for c in range(3):
            out_ref[c, x - HU] = jnp.concatenate(values[c], axis=0)[4 : 4 + CY]
        return carry

    lax.fori_loop(HU, HU + CX, last, 0, unroll=2)

    def send_field(i, d):
        copy_of(2, i, d).start()

    each(cross, send_field)
    each(same, send_field)

    def split_own(x, carry):
        for c in range(3):
            store_split(fm, (c, x, slice(None)), out_ref[c, x])
        return carry

    lax.fori_loop(0, CX, split_own, 0, unroll=2)

    def moments(blk, parts, first):
        weight = wz[blk]
        for c in range(3):
            sums = [jnp.zeros((8, 128), F32) for _ in range(4)]
            for ref, tiles, lead, xs in parts:
                field = ref[c] if len(ref.shape) == 3 else ref[c].reshape(CX * CY, KZ)
                product = jnp.dot(field, weight, preferred_element_type=F32)
                for n, x in enumerate(xs):
                    along0 = along1 = slope = bend = None
                    for t in range(tiles):
                        row = (n * tiles + t) * 8
                        t0, t1, t2 = [product[row : row + 8, i * 128 : i * 128 + 128] for i in range(3)]
                        g0, g1, g2 = [wy[blk, i, (lead + t) * 8 : (lead + t) * 8 + 8] for i in range(3)]
                        terms = t0 * g0, t1 * g0, t0 * g1, t0 * g2 + t2 * g0
                        if t == 0:
                            along0, along1, slope, bend = terms
                        else:
                            along0, along1, slope, bend = [p + q for p, q in zip((along0, along1, slope, bend), terms)]
                    x0, x1, x2 = [wx[blk, i, x : x + 1] for i in range(3)]
                    sums[0] += along0 * x1
                    sums[1] += slope * x0
                    sums[2] += along1 * x0
                    sums[3] += along0 * x2 + bend * x0
            for j, item in enumerate(sums):
                at = pl.ds((4 * c + j) * BLOCKS + blk, 1)
                item = jnp.sum(item, axis=0, keepdims=True)
                grad_ref[at] = item if first else grad_ref[at] + item

    def own_moments(blk, carry):
        moments(blk, ((fm, CY // 8, 0, range(4, 4 + CX)),), True)
        return carry

    lax.fori_loop(0, BLOCKS, own_moments, 0)

    each(exists, arrived((2,)))

    for c in range(3):
        store_split(fx, (c, slice(None)), xh[c].reshape(8 * YN, NZ))
        store_split(fy, (c, slice(None)), yh[c].reshape(8 * CX, NZ))

    def halo_moments(blk, carry):
        parts = (
            (fx, YN // 8, CY // 8, (*range(4), *range(20, 24))),
            (fy, 1, (CY + YN) // 8, range(4, 4 + CX)),
        )
        moments(blk, parts, False)
        return carry

    lax.fori_loop(0, BLOCKS, halo_moments, 0)

    def sent(i, d):
        for k in range(3):
            copy_of(k, i, d).wait_send()

    each(exists, sent)


def body(adjoint_velocity, coefficient, record_counts, record_cells, record_offsets):
    nw, nn = lax.axis_size("wide"), lax.axis_size("narrow")
    vmem = pl.BlockSpec(memory_space=pltpu.VMEM)
    hbm = pl.BlockSpec(memory_space=pltpu.HBM)
    smoothed, grads = pl.pallas_call(
        functools.partial(kernel, nw, nn),
        out_shape=(
            jax.ShapeDtypeStruct((3, CX, CY, NZ), F32),
            jax.ShapeDtypeStruct((12 * BLOCKS, 128), F32),
        ),
        in_specs=[hbm, hbm, pl.BlockSpec(memory_space=pltpu.SMEM), vmem, vmem],
        out_specs=(vmem, vmem),
        scratch_shapes=[
            pltpu.VMEM((3, XU, YB, NZ), F32),
            pltpu.VMEM((XC, YB, NZ), F32),
            pltpu.VMEM((3, XU, YB, NZ), F32),
            pltpu.VMEM((3, XU, YB, NZ), F32),
            pltpu.VMEM((3, XU, YB, NZ), F32),
            pltpu.VMEM((6, XU, YN, NZ), F32),
            pltpu.VMEM((3, 8, YN, NZ), F32),
            pltpu.VMEM((3, CX, 8, NZ), F32),
            pltpu.VMEM((3, CX, CY, KZ), BF16),
            pltpu.VMEM((3, 8 * YN, KZ), BF16),
            pltpu.VMEM((3, 8 * CX, KZ), BF16),
            pltpu.VMEM((BLOCKS, KZ, 384), BF16),
            pltpu.VMEM((BLOCKS, 3, CY + YN + 8, 128), F32),
            pltpu.VMEM((BLOCKS, 3, XW, 128), F32),
            pltpu.SemaphoreType.DMA((2,)),
            pltpu.SemaphoreType.DMA((3, 8)),
            pltpu.SemaphoreType.DMA((3, 8)),
            pltpu.SemaphoreType.REGULAR,
        ],
        compiler_params=pltpu.CompilerParams(
            collective_id=0, has_side_effects=True, vmem_limit_bytes=40 << 20
        ),
    )(
        adjoint_velocity,
        coefficient,
        record_counts,
        record_cells.reshape(3 * BLOCKS, 128),
        record_offsets.reshape(3 * BLOCKS, 128),
    )
    return smoothed, grads.reshape(1, 1, 12, SLOTS)


def solution(mesh):
    return jax.shard_map(
        body,
        mesh=mesh,
        in_specs=(
            P(None, "wide", "narrow", None),
            P("wide", "narrow", None),
            P("wide", "narrow"),
            P("wide", "narrow", None, None),
            P("wide", "narrow", None, None),
        ),
        out_specs=(P(None, "wide", "narrow", None), P("wide", "narrow", None, None)),
        check_vma=False,
    )
```

```python
import functools
import math

import jax
import jax.numpy as jnp
from jax import lax
from jax.experimental import pallas as pl
from jax.experimental.pallas import tpu as pltpu
from jax.sharding import PartitionSpec as P

MESH = pl.DeviceIdType.MESH
F32 = jnp.float32
BF16 = jnp.bfloat16

RADIUS = 4
CX, CY, NZ = 16, 32, 128
SLOTS = 1024
BLOCKS = SLOTS // 128
HU = 3
HC = 4
XU = CX + 2 * HU
XC = CX + 2 * HC
YA = 8
YN = CY + 8
Y0 = YA + 4
YB = YN + 16
TILES = YN // 8
KZ = 3 * NZ
FOREIGN = 7
PACKED = FOREIGN * 128
CLASSES = (
    ((-1, 0), 0, 256),
    ((1, 0), 256, 256),
    ((0, -1), 512, 128),
    ((0, 1), 640, 128),
    ((-1, -1), 768, 32),
    ((-1, 1), 800, 32),
    ((1, -1), 832, 32),
    ((1, 1), 864, 32),
)
CORNERS = ((-1, -1), (-1, 1), (1, -1), (1, 1))

WIDTH = 1.25
RELAX = 0.8

DIRS = [(dx, dy) for dx in (-1, 0, 1) for dy in (-1, 0, 1) if (dx, dy) != (0, 0)]


def profile(distance):
    width_sq = WIDTH * WIDTH
    base = jnp.exp(-distance * distance / (2.0 * width_sq)) / (WIDTH * math.sqrt(2.0 * math.pi))
    first = -distance / width_sq * base
    second = (distance * distance / width_sq - 1.0) / width_sq * base
    return (base, first, second)


def weights(places, centre, offset):
    distance = places - centre
    inside = jnp.abs(distance) <= RADIUS
    return [jnp.where(inside, item, 0.0) for item in profile(distance + 0.5 - offset)]


def split(value):
    high = value.astype(BF16)
    return high, (value - high.astype(F32)).astype(BF16)


def blocks_of(d, landing):
    if d[0] and d[1]:
        return pl.ds(6 + (CORNERS.index(d) if landing else 0), 1)
    return {(-1, 0): pl.ds(0, 2), (1, 0): pl.ds(2, 2), (0, -1): pl.ds(4, 1), (0, 1): pl.ds(5, 1)}[d]


def along(d, low, own, high):
    return (low, own, high)[d + 1]


def kernel(
    nw, nn, u_ref, k_ref, count_ref, cell_ref, off_ref, out_ref, grad_ref,
    ub, cb, w1, wa, wb, ck, fm, fe, wz, wy, wx, gm, dm, mine, theirs, part, back, total,
    own_sem, send_sem, recv_sem,
):
    a, b = lax.axis_index("wide"), lax.axis_index("narrow")
    half = nn // 2

    def exists(d):
        return (a + d[0] >= 0) & (a + d[0] < nw) & (b + d[1] >= 0) & (b + d[1] < nn)

    def same(d):
        if d[1] == 0:
            return exists(d)
        return exists(d) & ((b < half) == (b + d[1] < half))

    def cross(d):
        if d[1] == 0:
            return None
        return exists(d) & ((b < half) != (b + d[1] < half))

    def each(test, action):
        for i, d in enumerate(DIRS):
            ok = test(d)
            if ok is not None:
                pl.when(ok)(functools.partial(action, i, d))

    def number(test):
        return sum(jnp.where(test(d), 1, 0) for d in DIRS if test(d) is not None)

    def copy_of(k, i, d):
        x, y = d
        to = (a + x, b + y)

        def remote(k, src, dst):
            return pltpu.make_async_remote_copy(
                src_ref=src, dst_ref=dst, send_sem=send_sem.at[k, i], recv_sem=recv_sem.at[k, i],
                device_id=to, device_id_type=MESH,
            )

        def parts(n, lo_x, lo_y):
            src = (
                along(x, pl.ds(0, n), pl.ds(0, CX), pl.ds(CX - n, n)),
                along(y, pl.ds(0, n), pl.ds(0, CY), pl.ds(CY - n, n)),
            )
            dst = (
                along(x, pl.ds(lo_x + CX, n), pl.ds(lo_x, CX), pl.ds(lo_x - n, n)),
                along(y, pl.ds(lo_y + CY, n), pl.ds(lo_y, CY), pl.ds(lo_y - n, n)),
            )
            return src, dst

        if k == 0:
            src, dst = parts(HC, HC, Y0)
            return remote(k, k_ref.at[src], cb.at[dst])
        if k == 1:
            src, dst = parts(HU, HU, Y0)
            return remote(k, u_ref.at[:, src[0], src[1]], ub.at[:, dst[0], dst[1]])
        if k == 2:
            return remote(k, mine.at[blocks_of(d, False)], theirs.at[blocks_of(d, True)])
        came = (-x, -y)
        return remote(k, part.at[blocks_of(came, False)], back.at[blocks_of(came, True)])

    barrier = pltpu.get_barrier_semaphore()

    def signal(i, d):
        pl.semaphore_signal(barrier, inc=1, device_id=(a + d[0], b + d[1]), device_id_type=MESH)

    def send(i, d):
        for k in range(3):
            copy_of(k, i, d).start()

    each(exists, signal)
    own_k = pltpu.make_async_copy(k_ref, cb.at[pl.ds(HC, CX), pl.ds(Y0, CY)], own_sem.at[0])
    own_u = pltpu.make_async_copy(u_ref, ub.at[:, pl.ds(HU, CX), pl.ds(Y0, CY)], own_sem.at[1])
    own_k.start()
    own_u.start()

    @pl.when(a == 0)
    def _():
        ub[:, 0:HU] = jnp.zeros((3, HU, YB, NZ), F32)
        cb[0:HC] = jnp.zeros((HC, YB, NZ), F32)

    @pl.when(a == nw - 1)
    def _():
        ub[:, HU + CX :] = jnp.zeros((3, HU, YB, NZ), F32)
        cb[HC + CX :] = jnp.zeros((HC, YB, NZ), F32)

    @pl.when(b == 0)
    def _():
        ub[:, :, Y0 - 4 : Y0] = jnp.zeros((3, XU, 4, NZ), F32)
        cb[:, Y0 - 4 : Y0] = jnp.zeros((XC, 4, NZ), F32)

    @pl.when(b == nn - 1)
    def _():
        ub[:, :, Y0 + CY : Y0 + CY + 4] = jnp.zeros((3, XU, 4, NZ), F32)
        cb[:, Y0 + CY : Y0 + CY + 4] = jnp.zeros((XC, 4, NZ), F32)

    for d in DIRS:

        @pl.when(jnp.logical_not(exists(d)))
        def _():
            at, came = blocks_of(d, True), blocks_of((-d[0], -d[1]), True)
            back[at] = jnp.zeros((at.size, 16, 128), F32)
            theirs[came] = jnp.zeros((came.size, 8, 128), F32)

    lane1 = lax.broadcasted_iota(jnp.int32, (1, 128), 1)
    before = lax.broadcasted_iota(jnp.int32, (128, 128), 0) < lax.broadcasted_iota(jnp.int32, (128, 128), 1)
    before = jnp.where(before, 1.0, 0.0).astype(BF16)
    starts = jnp.concatenate([jnp.full((1, 128), first, F32) for _, first, _ in CLASSES], axis=0)

    def record(blk):
        centre = [cell_ref[pl.ds(d * BLOCKS + blk, 1)].astype(F32) for d in range(3)]
        offset = [off_ref[pl.ds(d * BLOCKS + blk, 1)] for d in range(3)]
        live = jnp.where(lane1 + blk * 128 < count_ref[0, 0], 1.0, 0.0)
        return centre, offset, live

    def pack(blk, seen):
        lanes = pl.ds(pl.multiple_of(blk * 128, 128), 128)
        centre, offset, live = record(blk)
        reach = {
            (0, -1): centre[0] < RADIUS, (0, 1): centre[0] >= CX - RADIUS,
            (1, -1): centre[1] < RADIUS, (1, 1): centre[1] >= CY - RADIUS,
        }
        member = []
        for d, _, _ in CLASSES:
            one = jnp.ones((1, 128), F32)
            for axis in range(2):
                if d[axis]:
                    one = jnp.where(reach[axis, d[axis]], one, 0.0)
            member.append(one)
        member = jnp.concatenate(member, axis=0)
        place = jnp.dot(member.astype(BF16), before, preferred_element_type=F32) + seen + starts
        place = jnp.where(member > 0.0, place, -1.0)
        for i, (_, first, size) in enumerate(CLASSES):
            rows = lax.broadcasted_iota(jnp.int32, (size, 128), 0).astype(F32) + float(first)
            gm[first : first + size, lanes] = jnp.where(rows == place[i : i + 1], 1.0, 0.0).astype(BF16)
        pieces = list(centre)
        rest = offset
        for _ in range(3):
            high = [item.astype(BF16).astype(F32) for item in rest]
            rest = [item - piece for item, piece in zip(rest, high)]
            pieces += high
        pieces += [live] + [jnp.zeros((1, 128), F32)] * 3
        dm[:, lanes] = jnp.concatenate(pieces, axis=0).astype(BF16)
        return seen + jnp.sum(member, axis=1, keepdims=True)

    lax.fori_loop(0, BLOCKS, pack, jnp.zeros((8, 128), F32))
    packed = lax.dot_general(dm[...], gm[...], (((1,), (1,)), ((), ())), preferred_element_type=F32)
    for f in range(FOREIGN):
        item = packed[:, f * 128 : f * 128 + 128]
        offset = item[3:6] + (item[6:9] + item[9:12])
        mine[f] = jnp.concatenate([item[0:3], offset, item[12:14]], axis=0)

    pl.semaphore_wait(barrier, number(exists))
    each(cross, send)
    each(same, send)

    def prepare(blk, centre, offset, live):
        rows = lax.broadcasted_iota(jnp.int32, (NZ, 128), 0).astype(F32)
        for i, item in enumerate(weights(rows, centre[2], offset[2])):
            high, low = split(item)
            wz[blk, 0:128, i * 128 : i * 128 + 128] = high
            wz[blk, 128:256, i * 128 : i * 128 + 128] = high
            wz[blk, 256:384, i * 128 : i * 128 + 128] = low
        rows = lax.broadcasted_iota(jnp.int32, (CY, 128), 0).astype(F32)
        for i, item in enumerate(weights(rows, centre[1], offset[1])):
            wy[blk, i] = item
        for i, item in enumerate(weights(rows[:CX], centre[0], offset[0])):
            wx[blk, i] = item * live

    def prepare_own(blk, carry):
        prepare(blk, *record(blk))
        return carry

    lax.fori_loop(0, BLOCKS, prepare_own, 0)

    def arrived(k):
        def action(i, d):
            j = DIRS.index((-d[0], -d[1]))
            copy_of(k, j, DIRS[j]).wait_recv()

        return action

    def corner(values):
        result = values[3]
        for i in (2, 1, 0):
            result = jnp.where(lane1 < 32 * (i + 1), values[i], result)
        return result

    each(exists, arrived(2))
    for f in range(FOREIGN):
        if f < 6:
            item = theirs[f]
            dx, dy = ((-1, 0), (-1, 0), (1, 0), (1, 0), (0, -1), (0, 1))[f]
            shift = -float(dx * CX), -float(dy * CY)
        else:
            item = corner([theirs[6 + i] for i in range(4)])
            shift = [corner([jnp.full((1, 128), -float(d[axis] * n), F32) for d in CORNERS]) for axis, n in ((0, CX), (1, CY))]
        centre = [item[0:1] + shift[0], item[1:2] + shift[1], item[2:3]]
        prepare(BLOCKS + f, centre, [item[3:4], item[4:5], item[5:6]], item[6:7])

    own_k.wait()
    own_u.wait()

    each(exists, arrived(0))
    each(exists, arrived(1))

    lane = lax.broadcasted_iota(jnp.int32, (8, NZ), 1)
    last_z, first_z = lane == NZ - 1, lane == 0
    y_at = lax.broadcasted_iota(jnp.int32, (8, NZ), 0) + (b * CY - 4)

    def face_coefficients(x, carry):
        x_at = a * CX - HU + x
        x_in = (x_at >= 0) & (x_at < nw * CX)
        for t in range(TILES):
            r = YA + 8 * t
            mid = cb[x + 1, r : r + 8]
            beside = [
                cb[x + 2, r : r + 8],
                cb[x, r : r + 8],
                cb[x + 1, r + 1 : r + 9],
                cb[x + 1, r - 1 : r + 7],
                jnp.where(last_z, 0.0, pltpu.roll(mid, NZ - 1, 1)),
                jnp.where(first_z, 0.0, pltpu.roll(mid, 1, 1)),
            ]
            faces = [0.5 * (mid + item) for item in beside]
            total = 1.0 + sum(faces)
            y = y_at + 8 * t
            scale = jnp.where((y >= 0) & (y < nn * CY) & x_in, RELAX / total, 0.0)
            faces[4] = jnp.where(last_z, 0.0, faces[4])
            faces[5] = jnp.where(first_z, 0.0, faces[5])
            for i, face in enumerate(faces):
                ck[i, x, 8 * t : 8 * t + 8] = scale * face
            for c in range(3):
                w1[c, x, r : r + 8] = scale * ub[c, x, r : r + 8]
        return carry

    lax.fori_loop(0, XU, face_coefficients, 0, unroll=2)

    def relaxed(src, x):
        values = [[], [], []]
        for t in range(TILES):
            r = YA + 8 * t
            k = [ck[i, x, 8 * t : 8 * t + 8] for i in range(6)]
            for c in range(3):
                mid = src[c, x, r : r + 8]
                total = (1.0 - RELAX) * mid + w1[c, x, r : r + 8]
                ends = k[4] * pltpu.roll(mid, NZ - 1, 1) + k[5] * pltpu.roll(mid, 1, 1)
                sides = k[2] * src[c, x, r + 1 : r + 9] + k[3] * src[c, x, r - 1 : r + 7]
                total += k[0] * src[c, x + 1, r : r + 8] + k[1] * src[c, x - 1, r : r + 8]
                values[c].append(total + sides + ends)
        return values

    def sweep(src, dst):
        def step(x, carry):
            values = relaxed(src, x)
            for c in range(3):
                for t in range(TILES):
                    dst[c, x, YA + 8 * t : YA + 8 * t + 8] = values[c][t]
            return carry

        return step

    lax.fori_loop(1, XU - 1, sweep(w1, wa), 0, unroll=2)
    lax.fori_loop(2, XU - 2, sweep(wa, wb), 0, unroll=2)

    def store_split(ref, index, value):
        high, low = split(value)
        ref[(*index, slice(0, 128))] = high
        ref[(*index, slice(128, 256))] = low
        ref[(*index, slice(256, 384))] = high

    def last(x, carry):
        values = relaxed(wb, x)
        for c in range(3):
            out_ref[c, x - HU] = jnp.concatenate(values[c], axis=0)[4 : 4 + CY]
        return carry

    lax.fori_loop(HU, HU + CX, last, 0, unroll=2)

    def split_own(x, carry):
        for c in range(3):
            field = out_ref[c, x]
            store_split(fm, (c, x, slice(None)), field)
            store_split(fe, (c, x, slice(None)), jnp.concatenate([field[:8], field[CY - 8 :]], axis=0))
        return carry

    lax.fori_loop(0, CX, split_own, 0, unroll=2)

    def contract(blk, product, row, xs, tiles, step):
        sums = [jnp.zeros((8, 128), F32) for _ in range(4)]
        for n, x in enumerate(xs):
            along0 = along1 = slope = bend = None
            for at, t in tiles:
                r = row + (n * step + at) * 8
                t0, t1, t2 = [product[r : r + 8, i * 128 : i * 128 + 128] for i in range(3)]
                g0, g1, g2 = [wy[blk, i, t * 8 : t * 8 + 8] for i in range(3)]
                terms = t0 * g0, t1 * g0, t0 * g1, t0 * g2 + t2 * g0
                if along0 is None:
                    along0, along1, slope, bend = terms
                else:
                    along0, along1, slope, bend = [p + q for p, q in zip((along0, along1, slope, bend), terms)]
            x0, x1, x2 = [wx[blk, i, x : x + 1] for i in range(3)]
            sums[0] += along0 * x1
            sums[1] += slope * x0
            sums[2] += along1 * x0
            sums[3] += along0 * x2 + bend * x0
        return [jnp.sum(item, axis=0, keepdims=True) for item in sums]

    own_tiles = tuple((t, t) for t in range(CY // 8))
    for f in range(FOREIGN):
        blk = BLOCKS + f
        if f < 4:
            xs, tiles, step = range(12, 16) if f < 2 else range(4), own_tiles, CY // 8
            field = fm[:, xs[0] : xs[0] + 4].reshape(3 * 4 * CY, KZ)
        elif f < 6:
            xs, tiles, step = range(CX), (((1, 3),), ((0, 0),))[f - 4], 2
            field = fe[...].reshape(3 * CX * 16, KZ)
        else:
            xs, tiles, step = (*range(4), *range(12, 16)), ((0, 0), (1, 3)), 2
            field = jnp.concatenate([fe[c, x : x + 4].reshape(64, KZ) for c in range(3) for x in (0, 12)], axis=0)
        product = jnp.dot(field, wz[blk], preferred_element_type=F32)
        rows = []
        for c in range(3):
            rows += contract(blk, product, c * len(xs) * step * 8, xs, tiles, step)
        part[f] = jnp.concatenate(rows + [jnp.zeros((4, 128), F32)], axis=0)

    def send_back(i, d):
        copy_of(3, i, d).start()

    each(cross, send_back)
    each(same, send_back)

    def own_moments(blk, carry):
        rows = []
        for c in range(3):
            product = jnp.dot(fm[c].reshape(CX * CY, KZ), wz[blk], preferred_element_type=F32)
            rows += contract(blk, product, 0, range(CX), own_tiles, CY // 8)
        lanes = pl.ds(pl.multiple_of(blk * 128, 128), 128)
        total[:, lanes] = jnp.concatenate(rows + [jnp.zeros((4, 128), F32)], axis=0)
        return carry

    lax.fori_loop(0, BLOCKS, own_moments, 0)

    each(exists, arrived(3))
    high, low = [], []
    for f in range(FOREIGN):
        item = back[f] if f < 6 else corner([back[6 + i] for i in range(4)])
        piece, rest = split(item)
        high.append(piece)
        low.append(rest)
    both = jnp.concatenate([jnp.concatenate(high, axis=1), jnp.concatenate(low, axis=1)], axis=0)
    spread = jnp.dot(both, gm[...], preferred_element_type=F32)
    grad_ref[0, 0] = (total[...] + (spread[:16] + spread[16:]))[:12]

    def sent(i, d):
        for k in range(4):
            copy_of(k, i, d).wait_send()

    each(exists, sent)


def body(adjoint_velocity, coefficient, record_counts, record_cells, record_offsets):
    nw, nn = lax.axis_size("wide"), lax.axis_size("narrow")
    vmem = pl.BlockSpec(memory_space=pltpu.VMEM)
    hbm = pl.BlockSpec(memory_space=pltpu.HBM)
    return pl.pallas_call(
        functools.partial(kernel, nw, nn),
        out_shape=(
            jax.ShapeDtypeStruct((3, CX, CY, NZ), F32),
            jax.ShapeDtypeStruct((1, 1, 12, SLOTS), F32),
        ),
        in_specs=[hbm, hbm, pl.BlockSpec(memory_space=pltpu.SMEM), vmem, vmem],
        out_specs=(vmem, vmem),
        scratch_shapes=[
            pltpu.VMEM((3, XU, YB, NZ), F32),
            pltpu.VMEM((XC, YB, NZ), F32),
            pltpu.VMEM((3, XU, YB, NZ), F32),
            pltpu.VMEM((3, XU, YB, NZ), F32),
            pltpu.VMEM((3, XU, YB, NZ), F32),
            pltpu.VMEM((6, XU, YN, NZ), F32),
            pltpu.VMEM((3, CX, CY, KZ), BF16),
            pltpu.VMEM((3, CX, 16, KZ), BF16),
            pltpu.VMEM((BLOCKS + FOREIGN, KZ, 384), BF16),
            pltpu.VMEM((BLOCKS + FOREIGN, 3, CY, 128), F32),
            pltpu.VMEM((BLOCKS + FOREIGN, 3, CX, 128), F32),
            pltpu.VMEM((PACKED, SLOTS), BF16),
            pltpu.VMEM((16, SLOTS), BF16),
            pltpu.VMEM((FOREIGN, 8, 128), F32),
            pltpu.VMEM((FOREIGN + 3, 8, 128), F32),
            pltpu.VMEM((FOREIGN, 16, 128), F32),
            pltpu.VMEM((FOREIGN + 3, 16, 128), F32),
            pltpu.VMEM((16, SLOTS), F32),
            pltpu.SemaphoreType.DMA((2,)),
            pltpu.SemaphoreType.DMA((4, 8)),
            pltpu.SemaphoreType.DMA((4, 8)),
        ],
        compiler_params=pltpu.CompilerParams(
            collective_id=0, has_side_effects=True, vmem_limit_bytes=40 << 20
        ),
    )(
        adjoint_velocity,
        coefficient,
        record_counts,
        record_cells.reshape(3 * BLOCKS, 128),
        record_offsets.reshape(3 * BLOCKS, 128),
    )


def solution(mesh):
    return jax.shard_map(
        body,
        mesh=mesh,
        in_specs=(
            P(None, "wide", "narrow", None),
            P("wide", "narrow", None),
            P("wide", "narrow"),
            P("wide", "narrow", None, None),
            P("wide", "narrow", None, None),
        ),
        out_specs=(P(None, "wide", "narrow", None), P("wide", "narrow", None, None)),
        check_vma=False,
    )
```

```python
import functools
import math

import jax
import jax.numpy as jnp
from jax import lax
from jax.experimental import pallas as pl
from jax.experimental.pallas import tpu as pltpu
from jax.sharding import PartitionSpec as P

MESH = pl.DeviceIdType.MESH
F32 = jnp.float32
BF16 = jnp.bfloat16

RADIUS = 4
CX, CY, NZ = 16, 32, 128
SLOTS = 1024
BLOCKS = SLOTS // 128
HU = 3
HC = 4
XU = CX + 2 * HU
XC = CX + 2 * HC
YA = 8
YN = CY + 8
Y0 = YA + 4
YB = YN + 16
TILES = YN // 8
KZ = 3 * NZ
FOREIGN = 7
PACKED = FOREIGN * 128
CLASSES = (
    ((-1, 0), 0, 256),
    ((1, 0), 256, 256),
    ((0, -1), 512, 128),
    ((0, 1), 640, 128),
    ((-1, -1), 768, 32),
    ((-1, 1), 800, 32),
    ((1, -1), 832, 32),
    ((1, 1), 864, 32),
)
CORNERS = ((-1, -1), (-1, 1), (1, -1), (1, 1))

WIDTH = 1.25
RELAX = 0.8

DIRS = [(dx, dy) for dx in (-1, 0, 1) for dy in (-1, 0, 1) if (dx, dy) != (0, 0)]


def profile(distance):
    width_sq = WIDTH * WIDTH
    base = jnp.exp(-distance * distance / (2.0 * width_sq)) / (WIDTH * math.sqrt(2.0 * math.pi))
    first = -distance / width_sq * base
    second = (distance * distance / width_sq - 1.0) / width_sq * base
    return (base, first, second)


def weights(places, centre, offset):
    distance = places - centre
    inside = jnp.abs(distance) <= RADIUS
    return [jnp.where(inside, item, 0.0) for item in profile(distance + 0.5 - offset)]


def split(value):
    high = value.astype(BF16)
    return high, (value - high.astype(F32)).astype(BF16)


def blocks_of(d, landing):
    if d[0] and d[1]:
        return pl.ds(6 + (CORNERS.index(d) if landing else 0), 1)
    return {(-1, 0): pl.ds(0, 2), (1, 0): pl.ds(2, 2), (0, -1): pl.ds(4, 1), (0, 1): pl.ds(5, 1)}[d]


def along(d, low, own, high):
    return (low, own, high)[d + 1]


def kernel(
    nw, nn, u_ref, k_ref, count_ref, cells, offsets, out, grad_ref,
    ub, cb, w1, wa, wb, ck, fm, fe, wz, wy, wx, gm, dm, mine, theirs, part, back, total, cell_ref, off_ref, out_ref,
    own_sem, send_sem, recv_sem,
):
    a, b = lax.axis_index("wide"), lax.axis_index("narrow")
    half = nn // 2

    def exists(d):
        return (a + d[0] >= 0) & (a + d[0] < nw) & (b + d[1] >= 0) & (b + d[1] < nn)

    def same(d):
        if d[1] == 0:
            return exists(d)
        return exists(d) & ((b < half) == (b + d[1] < half))

    def cross(d):
        if d[1] == 0:
            return None
        return exists(d) & ((b < half) != (b + d[1] < half))

    def each(test, action):
        for i, d in enumerate(DIRS):
            ok = test(d)
            if ok is not None:
                pl.when(ok)(functools.partial(action, i, d))

    def number(test):
        return sum(jnp.where(test(d), 1, 0) for d in DIRS if test(d) is not None)

    def copy_of(k, i, d):
        x, y = d
        to = (a + x, b + y)

        def remote(k, src, dst):
            return pltpu.make_async_remote_copy(
                src_ref=src, dst_ref=dst, send_sem=send_sem.at[k, i], recv_sem=recv_sem.at[k, i],
                device_id=to, device_id_type=MESH,
            )

        def parts(n, lo_x, lo_y):
            src = (
                along(x, pl.ds(lo_x, n), pl.ds(lo_x, CX), pl.ds(lo_x + CX - n, n)),
                along(y, pl.ds(lo_y, n), pl.ds(lo_y, CY), pl.ds(lo_y + CY - n, n)),
            )
            dst = (
                along(x, pl.ds(lo_x + CX, n), pl.ds(lo_x, CX), pl.ds(lo_x - n, n)),
                along(y, pl.ds(lo_y + CY, n), pl.ds(lo_y, CY), pl.ds(lo_y - n, n)),
            )
            return src, dst

        if k == 0:
            src, dst = parts(HC, HC, Y0)
            return remote(k, cb.at[src], cb.at[dst])
        if k == 1:
            src, dst = parts(HU, HU, Y0)
            return remote(k, ub.at[:, src[0], src[1]], ub.at[:, dst[0], dst[1]])
        if k == 2:
            return remote(k, mine.at[blocks_of(d, False)], theirs.at[blocks_of(d, True)])
        came = (-x, -y)
        return remote(k, part.at[blocks_of(came, False)], back.at[blocks_of(came, True)])

    barrier = pltpu.get_barrier_semaphore()

    def signal(i, d):
        pl.semaphore_signal(barrier, inc=1, device_id=(a + d[0], b + d[1]), device_id_type=MESH)

    def send(i, d):
        for k in range(3):
            copy_of(k, i, d).start()

    each(exists, signal)
    own_k = pltpu.make_async_copy(k_ref, cb.at[pl.ds(HC, CX), pl.ds(Y0, CY)], own_sem.at[0])
    own_u = pltpu.make_async_copy(u_ref, ub.at[:, pl.ds(HU, CX), pl.ds(Y0, CY)], own_sem.at[1])
    own_cells = pltpu.make_async_copy(cells, cell_ref, own_sem.at[2])
    own_offsets = pltpu.make_async_copy(offsets, off_ref, own_sem.at[3])
    for copy in (own_cells, own_offsets, own_k, own_u):
        copy.start()

    @pl.when(a == 0)
    def _():
        ub[:, 0:HU] = jnp.zeros((3, HU, YB, NZ), F32)
        cb[0:HC] = jnp.zeros((HC, YB, NZ), F32)

    @pl.when(a == nw - 1)
    def _():
        ub[:, HU + CX :] = jnp.zeros((3, HU, YB, NZ), F32)
        cb[HC + CX :] = jnp.zeros((HC, YB, NZ), F32)

    @pl.when(b == 0)
    def _():
        ub[:, :, Y0 - 4 : Y0] = jnp.zeros((3, XU, 4, NZ), F32)
        cb[:, Y0 - 4 : Y0] = jnp.zeros((XC, 4, NZ), F32)

    @pl.when(b == nn - 1)
    def _():
        ub[:, :, Y0 + CY : Y0 + CY + 4] = jnp.zeros((3, XU, 4, NZ), F32)
        cb[:, Y0 + CY : Y0 + CY + 4] = jnp.zeros((XC, 4, NZ), F32)

    for d in DIRS:

        @pl.when(jnp.logical_not(exists(d)))
        def _():
            at, came = blocks_of(d, True), blocks_of((-d[0], -d[1]), True)
            back[at] = jnp.zeros((at.size, 16, 128), F32)
            theirs[came] = jnp.zeros((came.size, 8, 128), F32)

    lane1 = lax.broadcasted_iota(jnp.int32, (1, 128), 1)
    before = lax.broadcasted_iota(jnp.int32, (128, 128), 0) < lax.broadcasted_iota(jnp.int32, (128, 128), 1)
    before = jnp.where(before, 1.0, 0.0).astype(BF16)
    starts = jnp.concatenate([jnp.full((1, 128), first, F32) for _, first, _ in CLASSES], axis=0)

    def record(blk):
        centre = [cell_ref[pl.ds(d * BLOCKS + blk, 1)].astype(F32) for d in range(3)]
        offset = [off_ref[pl.ds(d * BLOCKS + blk, 1)] for d in range(3)]
        live = jnp.where(lane1 + blk * 128 < count_ref[0, 0], 1.0, 0.0)
        return centre, offset, live

    def pack(blk, seen):
        lanes = pl.ds(pl.multiple_of(blk * 128, 128), 128)
        centre, offset, live = record(blk)
        reach = {
            (0, -1): centre[0] < RADIUS, (0, 1): centre[0] >= CX - RADIUS,
            (1, -1): centre[1] < RADIUS, (1, 1): centre[1] >= CY - RADIUS,
        }
        member = []
        for d, _, _ in CLASSES:
            one = jnp.ones((1, 128), F32)
            for axis in range(2):
                if d[axis]:
                    one = jnp.where(reach[axis, d[axis]], one, 0.0)
            member.append(one)
        member = jnp.concatenate(member, axis=0)
        place = jnp.dot(member.astype(BF16), before, preferred_element_type=F32) + seen + starts
        place = jnp.where(member > 0.0, place, -1.0)
        for i, (_, first, size) in enumerate(CLASSES):
            rows = lax.broadcasted_iota(jnp.int32, (size, 128), 0).astype(F32) + float(first)
            gm[first : first + size, lanes] = jnp.where(rows == place[i : i + 1], 1.0, 0.0).astype(BF16)
        pieces = list(centre)
        rest = offset
        for _ in range(3):
            high = [item.astype(BF16).astype(F32) for item in rest]
            rest = [item - piece for item, piece in zip(rest, high)]
            pieces += high
        pieces += [live] + [jnp.zeros((1, 128), F32)] * 3
        dm[:, lanes] = jnp.concatenate(pieces, axis=0).astype(BF16)
        return seen + jnp.sum(member, axis=1, keepdims=True)

    own_cells.wait()
    own_offsets.wait()
    lax.fori_loop(0, BLOCKS, pack, jnp.zeros((8, 128), F32))
    packed = lax.dot_general(dm[...], gm[...], (((1,), (1,)), ((), ())), preferred_element_type=F32)
    for f in range(FOREIGN):
        item = packed[:, f * 128 : f * 128 + 128]
        offset = item[3:6] + (item[6:9] + item[9:12])
        mine[f] = jnp.concatenate([item[0:3], offset, item[12:14]], axis=0)

    own_k.wait()
    own_u.wait()
    pl.semaphore_wait(barrier, number(exists))
    each(cross, send)
    each(same, send)

    def prepare(blk, centre, offset, live):
        def at(i):
            start = blk % 2 * 384 + i * 128
            return pl.ds(start if isinstance(blk, int) else pl.multiple_of(start, 128), 128)

        rows = lax.broadcasted_iota(jnp.int32, (NZ, 128), 0).astype(F32)
        for i, item in enumerate(weights(rows, centre[2], offset[2])):
            high, low = split(item)
            wz[blk // 2, 0:128, at(i)] = high
            wz[blk // 2, 128:256, at(i)] = high
            wz[blk // 2, 256:384, at(i)] = low
        rows = lax.broadcasted_iota(jnp.int32, (CY, 128), 0).astype(F32)
        for i, item in enumerate(weights(rows, centre[1], offset[1])):
            wy[blk, i] = item
        for i, item in enumerate(weights(rows[:CX], centre[0], offset[0])):
            wx[blk, i] = item * live

    def prepare_own(blk, carry):
        prepare(blk, *record(blk))
        return carry

    lax.fori_loop(0, BLOCKS, prepare_own, 0)

    def arrived(k):
        def action(i, d):
            j = DIRS.index((-d[0], -d[1]))
            copy_of(k, j, DIRS[j]).wait_recv()

        return action

    def corner(values):
        result = values[3]
        for i in (2, 1, 0):
            result = jnp.where(lane1 < 32 * (i + 1), values[i], result)
        return result

    each(exists, arrived(2))
    for f in range(FOREIGN):
        if f < 6:
            item = theirs[f]
            dx, dy = ((-1, 0), (-1, 0), (1, 0), (1, 0), (0, -1), (0, 1))[f]
            shift = -float(dx * CX), -float(dy * CY)
        else:
            item = corner([theirs[6 + i] for i in range(4)])
            shift = [corner([jnp.full((1, 128), -float(d[axis] * n), F32) for d in CORNERS]) for axis, n in ((0, CX), (1, CY))]
        centre = [item[0:1] + shift[0], item[1:2] + shift[1], item[2:3]]
        prepare(BLOCKS + f, centre, [item[3:4], item[4:5], item[5:6]], item[6:7])


    each(exists, arrived(0))
    each(exists, arrived(1))

    lane = lax.broadcasted_iota(jnp.int32, (8, NZ), 1)
    last_z, first_z = lane == NZ - 1, lane == 0
    y_at = lax.broadcasted_iota(jnp.int32, (8, NZ), 0) + (b * CY - 4)

    def face_coefficients(x, carry):
        x_at = a * CX - HU + x
        x_in = (x_at >= 0) & (x_at < nw * CX)
        for t in range(TILES):
            r = YA + 8 * t
            mid = cb[x + 1, r : r + 8]
            beside = [
                cb[x + 2, r : r + 8],
                cb[x, r : r + 8],
                cb[x + 1, r + 1 : r + 9],
                cb[x + 1, r - 1 : r + 7],
                jnp.where(last_z, 0.0, pltpu.roll(mid, NZ - 1, 1)),
                jnp.where(first_z, 0.0, pltpu.roll(mid, 1, 1)),
            ]
            faces = [0.5 * (mid + item) for item in beside]
            total = 1.0 + sum(faces)
            y = y_at + 8 * t
            scale = jnp.where((y >= 0) & (y < nn * CY) & x_in, RELAX / total, 0.0)
            faces[4] = jnp.where(last_z, 0.0, faces[4])
            faces[5] = jnp.where(first_z, 0.0, faces[5])
            for i, face in enumerate(faces):
                ck[i, x, 8 * t : 8 * t + 8] = scale * face
            for c in range(3):
                w1[c, x, r : r + 8] = scale * ub[c, x, r : r + 8]
        return carry

    lax.fori_loop(0, XU, face_coefficients, 0, unroll=2)

    def relaxed(src, x):
        values = [[], [], []]
        for t in range(TILES):
            r = YA + 8 * t
            k = [ck[i, x, 8 * t : 8 * t + 8] for i in range(6)]
            for c in range(3):
                mid = src[c, x, r : r + 8]
                total = (1.0 - RELAX) * mid + w1[c, x, r : r + 8]
                ends = k[4] * pltpu.roll(mid, NZ - 1, 1) + k[5] * pltpu.roll(mid, 1, 1)
                sides = k[2] * src[c, x, r + 1 : r + 9] + k[3] * src[c, x, r - 1 : r + 7]
                total += k[0] * src[c, x + 1, r : r + 8] + k[1] * src[c, x - 1, r : r + 8]
                values[c].append(total + sides + ends)
        return values

    def sweep(src, dst):
        def step(x, carry):
            values = relaxed(src, x)
            for c in range(3):
                for t in range(TILES):
                    dst[c, x, YA + 8 * t : YA + 8 * t + 8] = values[c][t]
            return carry

        return step

    lax.fori_loop(1, XU - 1, sweep(w1, wa), 0, unroll=10)
    lax.fori_loop(2, XU - 2, sweep(wa, wb), 0, unroll=9)

    def store_split(ref, index, value):
        high, low = split(value)
        ref[(*index, slice(0, 128))] = high
        ref[(*index, slice(128, 256))] = low
        ref[(*index, slice(256, 384))] = high

    def last(x, carry):
        values = relaxed(wb, x)
        for c in range(3):
            out_ref[c, x - HU] = jnp.concatenate(values[c], axis=0)[4 : 4 + CY]
        return carry

    lax.fori_loop(HU, HU + CX, last, 0, unroll=8)

    own_out = pltpu.make_async_copy(out_ref, out, own_sem.at[4])
    own_out.start()

    def split_own(x, carry):
        for c in range(3):
            field = out_ref[c, x]
            store_split(fm, (c, x, slice(None)), field)
            store_split(fe, (c, x, slice(None)), jnp.concatenate([field[:8], field[CY - 8 :]], axis=0))
        return carry

    lax.fori_loop(0, CX, split_own, 0, unroll=4)

    def contract(blk, product, row, xs, tiles, step, lead):
        sums = [jnp.zeros((8, 128), F32) for _ in range(4)]
        for n, x in enumerate(xs):
            along0 = along1 = slope = bend = None
            for at, t in tiles:
                r = row + (n * step + at) * 8
                t0, t1, t2 = [product[r : r + 8, lead + i * 128 : lead + i * 128 + 128] for i in range(3)]
                g0, g1, g2 = [wy[blk, i, t * 8 : t * 8 + 8] for i in range(3)]
                terms = t0 * g0, t1 * g0, t0 * g1, t0 * g2 + t2 * g0
                if along0 is None:
                    along0, along1, slope, bend = terms
                else:
                    along0, along1, slope, bend = [p + q for p, q in zip((along0, along1, slope, bend), terms)]
            x0, x1, x2 = [wx[blk, i, x : x + 1] for i in range(3)]
            sums[0] += along0 * x1
            sums[1] += slope * x0
            sums[2] += along1 * x0
            sums[3] += along0 * x2 + bend * x0
        return [jnp.sum(item, axis=0, keepdims=True) for item in sums]

    own_tiles = tuple((t, t) for t in range(CY // 8))
    for f in range(FOREIGN):
        blk = BLOCKS + f
        if f < 4:
            xs, tiles, step = range(12, 16) if f < 2 else range(4), own_tiles, CY // 8
            field = fm[:, xs[0] : xs[0] + 4].reshape(3 * 4 * CY, KZ)
        elif f < 6:
            xs, tiles, step = range(CX), (((1, 3),), ((0, 0),))[f - 4], 2
            field = fe[...].reshape(3 * CX * 16, KZ)
        else:
            xs, tiles, step = (*range(4), *range(12, 16)), ((0, 0), (1, 3)), 2
            field = jnp.concatenate([fe[c, x : x + 4].reshape(64, KZ) for c in range(3) for x in (0, 12)], axis=0)
        lead = f % 2 * 384
        if f == 6:
            product = jnp.dot(field, wz[blk // 2, :, 0:384], preferred_element_type=F32)
        elif f % 2 == 0:
            product = jnp.dot(field, wz[blk // 2], preferred_element_type=F32)
        rows = []
        for c in range(3):
            rows += contract(blk, product, c * len(xs) * step * 8, xs, tiles, step, lead)
        part[f] = jnp.concatenate(rows + [jnp.zeros((4, 128), F32)], axis=0)

    def send_back(i, d):
        copy_of(3, i, d).start()

    each(cross, send_back)
    each(same, send_back)

    def own_moments(pair, carry):
        rows = [[], []]
        for c in range(3):
            product = jnp.dot(fm[c].reshape(CX * CY, KZ), wz[pair], preferred_element_type=F32)
            for i in range(2):
                rows[i] += contract(pair * 2 + i, product, 0, range(CX), own_tiles, CY // 8, i * 384)
        for i in range(2):
            lanes = pl.ds(pl.multiple_of(pair * 256 + i * 128, 128), 128)
            total[:, lanes] = jnp.concatenate(rows[i] + [jnp.zeros((4, 128), F32)], axis=0)
        return carry

    lax.fori_loop(0, BLOCKS // 2, own_moments, 0)

    each(exists, arrived(3))
    high, low = [], []
    for f in range(FOREIGN):
        item = back[f] if f < 6 else corner([back[6 + i] for i in range(4)])
        piece, rest = split(item)
        high.append(piece)
        low.append(rest)
    both = jnp.concatenate([jnp.concatenate(high, axis=1), jnp.concatenate(low, axis=1)], axis=0)
    spread = jnp.dot(both, gm[...], preferred_element_type=F32)
    sums = total[...] + (spread[:16] + spread[16:])
    for blk in range(BLOCKS):
        grad_ref[pl.ds(blk, 12, stride=BLOCKS)] = sums[:12, blk * 128 : blk * 128 + 128]
    own_out.wait()

    def sent(i, d):
        for k in range(4):
            copy_of(k, i, d).wait_send()

    each(exists, sent)


def body(adjoint_velocity, coefficient, record_counts, record_cells, record_offsets):
    nw, nn = lax.axis_size("wide"), lax.axis_size("narrow")
    vmem = pl.BlockSpec(memory_space=pltpu.VMEM)
    hbm = pl.BlockSpec(memory_space=pl.ANY)
    smoothed, grads = pl.pallas_call(
        functools.partial(kernel, nw, nn),
        out_shape=(
            jax.ShapeDtypeStruct((3, CX, CY, NZ), F32),
            jax.ShapeDtypeStruct((12 * BLOCKS, 128), F32),
        ),
        in_specs=[hbm, hbm, pl.BlockSpec(memory_space=pltpu.SMEM), hbm, hbm],
        out_specs=(hbm, vmem),
        scratch_shapes=[
            pltpu.VMEM((3, XU, YB, NZ), F32),
            pltpu.VMEM((XC, YB, NZ), F32),
            pltpu.VMEM((3, XU, YB, NZ), F32),
            pltpu.VMEM((3, XU, YB, NZ), F32),
            pltpu.VMEM((3, XU, YB, NZ), F32),
            pltpu.VMEM((6, XU, YN, NZ), F32),
            pltpu.VMEM((3, CX, CY, KZ), BF16),
            pltpu.VMEM((3, CX, 16, KZ), BF16),
            pltpu.VMEM(((BLOCKS + FOREIGN + 1) // 2, KZ, 768), BF16),
            pltpu.VMEM((BLOCKS + FOREIGN, 3, CY, 128), F32),
            pltpu.VMEM((BLOCKS + FOREIGN, 3, CX, 128), F32),
            pltpu.VMEM((PACKED, SLOTS), BF16),
            pltpu.VMEM((16, SLOTS), BF16),
            pltpu.VMEM((FOREIGN, 8, 128), F32),
            pltpu.VMEM((FOREIGN + 3, 8, 128), F32),
            pltpu.VMEM((FOREIGN, 16, 128), F32),
            pltpu.VMEM((FOREIGN + 3, 16, 128), F32),
            pltpu.VMEM((16, SLOTS), F32),
            pltpu.VMEM((3 * BLOCKS, 128), jnp.int32),
            pltpu.VMEM((3 * BLOCKS, 128), F32),
            pltpu.VMEM((3, CX, CY, NZ), F32),
            pltpu.SemaphoreType.DMA((5,)),
            pltpu.SemaphoreType.DMA((4, 8)),
            pltpu.SemaphoreType.DMA((4, 8)),
        ],
        compiler_params=pltpu.CompilerParams(
            collective_id=0, has_side_effects=True, vmem_limit_bytes=63 << 20
        ),
    )(
        adjoint_velocity,
        coefficient,
        record_counts,
        record_cells.reshape(3 * BLOCKS, 128),
        record_offsets.reshape(3 * BLOCKS, 128),
    )
    return smoothed, grads.reshape(1, 1, 12, SLOTS)


def solution(mesh):
    return jax.shard_map(
        body,
        mesh=mesh,
        in_specs=(
            P(None, "wide", "narrow", None),
            P("wide", "narrow", None),
            P("wide", "narrow"),
            P("wide", "narrow", None, None),
            P("wide", "narrow", None, None),
        ),
        out_specs=(P(None, "wide", "narrow", None), P("wide", "narrow", None, None)),
        check_vma=False,
    )
```

```python
import functools
import math

import jax
import jax.numpy as jnp
from jax import lax
from jax.experimental import pallas as pl
from jax.experimental.pallas import tpu as pltpu
from jax.sharding import PartitionSpec as P

MESH = pl.DeviceIdType.MESH
F32 = jnp.float32
BF16 = jnp.bfloat16

RADIUS = 4
CX, CY, NZ = 16, 32, 128
SLOTS = 1024
BLOCKS = SLOTS // 128
HU = 3
HC = 4
XU = CX + 2 * HU
XC = CX + 2 * HC
YA = 8
YN = CY + 8
Y0 = YA + 4
YB = YN + 16
TILES = YN // 8
KZ = 3 * NZ
FOREIGN = 7
PACKED = FOREIGN * 128
CLASSES = (
    ((-1, 0), 0, 256),
    ((1, 0), 256, 256),
    ((0, -1), 512, 128),
    ((0, 1), 640, 128),
    ((-1, -1), 768, 32),
    ((-1, 1), 800, 32),
    ((1, -1), 832, 32),
    ((1, 1), 864, 32),
)
CORNERS = ((-1, -1), (-1, 1), (1, -1), (1, 1))

WIDTH = 1.25
RELAX = 0.8

DIRS = [(dx, dy) for dx in (-1, 0, 1) for dy in (-1, 0, 1) if (dx, dy) != (0, 0)]


def profile(distance):
    width_sq = WIDTH * WIDTH
    base = jnp.exp(-distance * distance / (2.0 * width_sq)) / (WIDTH * math.sqrt(2.0 * math.pi))
    first = -distance / width_sq * base
    second = (distance * distance / width_sq - 1.0) / width_sq * base
    return (base, first, second)


def weights(places, centre, offset):
    distance = places - centre
    inside = jnp.abs(distance) <= RADIUS
    return [jnp.where(inside, item, 0.0) for item in profile(distance + 0.5 - offset)]


def split(value):
    high = value.astype(BF16)
    return high, (value - high.astype(F32)).astype(BF16)


def blocks_of(d, landing):
    if d[0] and d[1]:
        return pl.ds(6 + (CORNERS.index(d) if landing else 0), 1)
    return {(-1, 0): pl.ds(0, 2), (1, 0): pl.ds(2, 2), (0, -1): pl.ds(4, 1), (0, 1): pl.ds(5, 1)}[d]


def along(d, low, own, high):
    return (low, own, high)[d + 1]


def kernel(
    nw, nn, u_ref, k_ref, counts, cells, offsets, out, grad_ref,
    ub, cb, w1, wa, wb, ck, fm, fe, wz, wy, wx, gm, dm, mine, theirs, part, back, total, count_ref, cell_ref, off_ref, out_ref,
    own_sem, send_sem, recv_sem,
):
    a, b = lax.axis_index("wide"), lax.axis_index("narrow")
    half = nn // 2

    def exists(d):
        return (a + d[0] >= 0) & (a + d[0] < nw) & (b + d[1] >= 0) & (b + d[1] < nn)

    def same(d):
        if d[1] == 0:
            return exists(d)
        return exists(d) & ((b < half) == (b + d[1] < half))

    def cross(d):
        if d[1] == 0:
            return None
        return exists(d) & ((b < half) != (b + d[1] < half))

    def each(test, action):
        for i, d in enumerate(DIRS):
            ok = test(d)
            if ok is not None:
                pl.when(ok)(functools.partial(action, i, d))

    def number(test):
        return sum(jnp.where(test(d), 1, 0) for d in DIRS if test(d) is not None)

    def copy_of(k, i, d):
        x, y = d
        to = (a + x, b + y)

        def remote(k, src, dst):
            return pltpu.make_async_remote_copy(
                src_ref=src, dst_ref=dst, send_sem=send_sem.at[k, i], recv_sem=recv_sem.at[k, i],
                device_id=to, device_id_type=MESH,
            )

        def parts(n, lo_x, lo_y):
            src = (
                along(x, pl.ds(lo_x, n), pl.ds(lo_x, CX), pl.ds(lo_x + CX - n, n)),
                along(y, pl.ds(lo_y, n), pl.ds(lo_y, CY), pl.ds(lo_y + CY - n, n)),
            )
            dst = (
                along(x, pl.ds(lo_x + CX, n), pl.ds(lo_x, CX), pl.ds(lo_x - n, n)),
                along(y, pl.ds(lo_y + CY, n), pl.ds(lo_y, CY), pl.ds(lo_y - n, n)),
            )
            return src, dst

        if k == 0:
            src, dst = parts(HC, HC, Y0)
            return remote(k, cb.at[src], cb.at[dst])
        if k == 1:
            src, dst = parts(HU, HU, Y0)
            return remote(k, ub.at[:, src[0], src[1]], ub.at[:, dst[0], dst[1]])
        if k == 2:
            return remote(k, mine.at[blocks_of(d, False)], theirs.at[blocks_of(d, True)])
        came = (-x, -y)
        return remote(k, part.at[blocks_of(came, False)], back.at[blocks_of(came, True)])

    barrier = pltpu.get_barrier_semaphore()

    def signal(i, d):
        pl.semaphore_signal(barrier, inc=1, device_id=(a + d[0], b + d[1]), device_id_type=MESH)

    def send(i, d):
        for k in range(3):
            copy_of(k, i, d).start()

    each(exists, signal)
    own_k = pltpu.make_async_copy(k_ref, cb.at[pl.ds(HC, CX), pl.ds(Y0, CY)], own_sem.at[0])
    own_u = pltpu.make_async_copy(u_ref, ub.at[:, pl.ds(HU, CX), pl.ds(Y0, CY)], own_sem.at[1])
    own_cells = pltpu.make_async_copy(cells, cell_ref, own_sem.at[2])
    own_offsets = pltpu.make_async_copy(offsets, off_ref, own_sem.at[3])
    own_count = pltpu.make_async_copy(counts, count_ref, own_sem.at[5])
    for copy in (own_count, own_cells, own_offsets, own_k, own_u):
        copy.start()

    @pl.when(a == 0)
    def _():
        ub[:, 0:HU] = jnp.zeros((3, HU, YB, NZ), F32)
        cb[0:HC] = jnp.zeros((HC, YB, NZ), F32)

    @pl.when(a == nw - 1)
    def _():
        ub[:, HU + CX :] = jnp.zeros((3, HU, YB, NZ), F32)
        cb[HC + CX :] = jnp.zeros((HC, YB, NZ), F32)

    @pl.when(b == 0)
    def _():
        ub[:, :, Y0 - 4 : Y0] = jnp.zeros((3, XU, 4, NZ), F32)
        cb[:, Y0 - 4 : Y0] = jnp.zeros((XC, 4, NZ), F32)

    @pl.when(b == nn - 1)
    def _():
        ub[:, :, Y0 + CY : Y0 + CY + 4] = jnp.zeros((3, XU, 4, NZ), F32)
        cb[:, Y0 + CY : Y0 + CY + 4] = jnp.zeros((XC, 4, NZ), F32)

    for d in DIRS:

        @pl.when(jnp.logical_not(exists(d)))
        def _():
            at, came = blocks_of(d, True), blocks_of((-d[0], -d[1]), True)
            back[at] = jnp.zeros((at.size, 16, 128), F32)
            theirs[came] = jnp.zeros((came.size, 8, 128), F32)

    lane1 = lax.broadcasted_iota(jnp.int32, (1, 128), 1)
    before = lax.broadcasted_iota(jnp.int32, (128, 128), 0) < lax.broadcasted_iota(jnp.int32, (128, 128), 1)
    before = jnp.where(before, 1.0, 0.0).astype(BF16)
    starts = jnp.concatenate([jnp.full((1, 128), first, F32) for _, first, _ in CLASSES], axis=0)

    def record(blk):
        centre = [cell_ref[pl.ds(d * BLOCKS + blk, 1)].astype(F32) for d in range(3)]
        offset = [off_ref[pl.ds(d * BLOCKS + blk, 1)] for d in range(3)]
        live = jnp.where(lane1 + blk * 128 < count_ref[...], 1.0, 0.0)
        return centre, offset, live

    def pack(blk, seen):
        lanes = pl.ds(pl.multiple_of(blk * 128, 128), 128)
        centre, offset, live = record(blk)
        reach = {
            (0, -1): centre[0] < RADIUS, (0, 1): centre[0] >= CX - RADIUS,
            (1, -1): centre[1] < RADIUS, (1, 1): centre[1] >= CY - RADIUS,
        }
        member = []
        for d, _, _ in CLASSES:
            one = jnp.ones((1, 128), F32)
            for axis in range(2):
                if d[axis]:
                    one = jnp.where(reach[axis, d[axis]], one, 0.0)
            member.append(one)
        member = jnp.concatenate(member, axis=0)
        place = jnp.dot(member.astype(BF16), before, preferred_element_type=F32) + seen + starts
        place = jnp.where(member > 0.0, place, -1.0)
        for i, (_, first, size) in enumerate(CLASSES):
            rows = lax.broadcasted_iota(jnp.int32, (size, 128), 0).astype(F32) + float(first)
            gm[first : first + size, lanes] = jnp.where(rows == place[i : i + 1], 1.0, 0.0).astype(BF16)
        pieces = list(centre)
        rest = offset
        for _ in range(3):
            high = [item.astype(BF16).astype(F32) for item in rest]
            rest = [item - piece for item, piece in zip(rest, high)]
            pieces += high
        pieces += [live] + [jnp.zeros((1, 128), F32)] * 3
        dm[:, lanes] = jnp.concatenate(pieces, axis=0).astype(BF16)
        return seen + jnp.sum(member, axis=1, keepdims=True)

    own_count.wait()
    own_cells.wait()
    own_offsets.wait()
    lax.fori_loop(0, BLOCKS, pack, jnp.zeros((8, 128), F32))
    packed = lax.dot_general(dm[...], gm[...], (((1,), (1,)), ((), ())), preferred_element_type=F32)
    for f in range(FOREIGN):
        item = packed[:, f * 128 : f * 128 + 128]
        offset = item[3:6] + (item[6:9] + item[9:12])
        mine[f] = jnp.concatenate([item[0:3], offset, item[12:14]], axis=0)

    own_k.wait()
    own_u.wait()
    pl.semaphore_wait(barrier, number(exists))
    each(cross, send)
    each(same, send)

    def prepare(blk, centre, offset, live):
        def at(i):
            start = blk % 2 * 384 + i * 128
            return pl.ds(start if isinstance(blk, int) else pl.multiple_of(start, 128), 128)

        rows = lax.broadcasted_iota(jnp.int32, (NZ, 128), 0).astype(F32)
        for i, item in enumerate(weights(rows, centre[2], offset[2])):
            high, low = split(item)
            wz[blk // 2, 0:128, at(i)] = high
            wz[blk // 2, 128:256, at(i)] = high
            wz[blk // 2, 256:384, at(i)] = low
        rows = lax.broadcasted_iota(jnp.int32, (CY, 128), 0).astype(F32)
        for i, item in enumerate(weights(rows, centre[1], offset[1])):
            wy[blk, i] = item
        for i, item in enumerate(weights(rows[:CX], centre[0], offset[0])):
            wx[blk, i] = item * live

    def prepare_own(blk, carry):
        prepare(blk, *record(blk))
        return carry

    lax.fori_loop(0, BLOCKS, prepare_own, 0)

    def arrived(k):
        def action(i, d):
            j = DIRS.index((-d[0], -d[1]))
            copy_of(k, j, DIRS[j]).wait_recv()

        return action

    def corner(values):
        result = values[3]
        for i in (2, 1, 0):
            result = jnp.where(lane1 < 32 * (i + 1), values[i], result)
        return result

    each(exists, arrived(2))
    for f in range(FOREIGN):
        if f < 6:
            item = theirs[f]
            dx, dy = ((-1, 0), (-1, 0), (1, 0), (1, 0), (0, -1), (0, 1))[f]
            shift = -float(dx * CX), -float(dy * CY)
        else:
            item = corner([theirs[6 + i] for i in range(4)])
            shift = [corner([jnp.full((1, 128), -float(d[axis] * n), F32) for d in CORNERS]) for axis, n in ((0, CX), (1, CY))]
        centre = [item[0:1] + shift[0], item[1:2] + shift[1], item[2:3]]
        prepare(BLOCKS + f, centre, [item[3:4], item[4:5], item[5:6]], item[6:7])


    each(exists, arrived(0))
    each(exists, arrived(1))

    lane = lax.broadcasted_iota(jnp.int32, (8, NZ), 1)
    last_z, first_z = lane == NZ - 1, lane == 0
    y_at = lax.broadcasted_iota(jnp.int32, (8, NZ), 0) + (b * CY - 4)

    def face_coefficients(x, carry):
        x_at = a * CX - HU + x
        x_in = (x_at >= 0) & (x_at < nw * CX)
        for t in range(TILES):
            r = YA + 8 * t
            mid = cb[x + 1, r : r + 8]
            beside = [
                cb[x + 2, r : r + 8],
                cb[x, r : r + 8],
                cb[x + 1, r + 1 : r + 9],
                cb[x + 1, r - 1 : r + 7],
                jnp.where(last_z, 0.0, pltpu.roll(mid, NZ - 1, 1)),
                jnp.where(first_z, 0.0, pltpu.roll(mid, 1, 1)),
            ]
            faces = [0.5 * (mid + item) for item in beside]
            total = 1.0 + sum(faces)
            y = y_at + 8 * t
            scale = jnp.where((y >= 0) & (y < nn * CY) & x_in, RELAX / total, 0.0)
            faces[4] = jnp.where(last_z, 0.0, faces[4])
            faces[5] = jnp.where(first_z, 0.0, faces[5])
            for i, face in enumerate(faces):
                ck[i, x, 8 * t : 8 * t + 8] = scale * face
            for c in range(3):
                w1[c, x, r : r + 8] = scale * ub[c, x, r : r + 8]
        return carry

    lax.fori_loop(0, XU, face_coefficients, 0, unroll=11)

    def relaxed(src, x):
        values = [[], [], []]
        for t in range(TILES):
            r = YA + 8 * t
            k = [ck[i, x, 8 * t : 8 * t + 8] for i in range(6)]
            for c in range(3):
                mid = src[c, x, r : r + 8]
                total = (1.0 - RELAX) * mid + w1[c, x, r : r + 8]
                ends = k[4] * pltpu.roll(mid, NZ - 1, 1) + k[5] * pltpu.roll(mid, 1, 1)
                sides = k[2] * src[c, x, r + 1 : r + 9] + k[3] * src[c, x, r - 1 : r + 7]
                total += k[0] * src[c, x + 1, r : r + 8] + k[1] * src[c, x - 1, r : r + 8]
                values[c].append(total + sides + ends)
        return values

    def sweep(src, dst):
        def step(x, carry):
            values = relaxed(src, x)
            for c in range(3):
                for t in range(TILES):
                    dst[c, x, YA + 8 * t : YA + 8 * t + 8] = values[c][t]
            return carry

        return step

    lax.fori_loop(1, XU - 1, sweep(w1, wa), 0, unroll=10)
    lax.fori_loop(2, XU - 2, sweep(wa, wb), 0, unroll=9)

    def store_split(ref, index, value):
        high, low = split(value)
        ref[(*index, slice(0, 128))] = high
        ref[(*index, slice(128, 256))] = low
        ref[(*index, slice(256, 384))] = high

    def last(x, carry):
        values = relaxed(wb, x)
        for c in range(3):
            out_ref[c, x - HU] = jnp.concatenate(values[c], axis=0)[4 : 4 + CY]
        return carry

    lax.fori_loop(HU, HU + CX, last, 0, unroll=8)

    own_out = pltpu.make_async_copy(out_ref, out, own_sem.at[4])
    own_out.start()

    def split_own(x, carry):
        for c in range(3):
            field = out_ref[c, x]
            store_split(fm, (c, x, slice(None)), field)
            store_split(fe, (c, x, slice(None)), jnp.concatenate([field[:8], field[CY - 8 :]], axis=0))
        return carry

    lax.fori_loop(0, CX, split_own, 0, unroll=8)

    def contract(blk, product, row, xs, tiles, step, lead):
        sums = [jnp.zeros((8, 128), F32) for _ in range(4)]
        for n, x in enumerate(xs):
            along0 = along1 = slope = bend = None
            for at, t in tiles:
                r = row + (n * step + at) * 8
                t0, t1, t2 = [product[r : r + 8, lead + i * 128 : lead + i * 128 + 128] for i in range(3)]
                g0, g1, g2 = [wy[blk, i, t * 8 : t * 8 + 8] for i in range(3)]
                terms = t0 * g0, t1 * g0, t0 * g1, t0 * g2 + t2 * g0
                if along0 is None:
                    along0, along1, slope, bend = terms
                else:
                    along0, along1, slope, bend = [p + q for p, q in zip((along0, along1, slope, bend), terms)]
            x0, x1, x2 = [wx[blk, i, x : x + 1] for i in range(3)]
            sums[0] += along0 * x1
            sums[1] += slope * x0
            sums[2] += along1 * x0
            sums[3] += along0 * x2 + bend * x0
        return [jnp.sum(item, axis=0, keepdims=True) for item in sums]

    own_tiles = tuple((t, t) for t in range(CY // 8))
    for f in range(FOREIGN):
        blk = BLOCKS + f
        if f < 4:
            xs, tiles, step = range(12, 16) if f < 2 else range(4), own_tiles, CY // 8
            field = fm[:, xs[0] : xs[0] + 4].reshape(3 * 4 * CY, KZ)
        elif f < 6:
            xs, tiles, step = range(CX), (((1, 3),), ((0, 0),))[f - 4], 2
            field = fe[...].reshape(3 * CX * 16, KZ)
        else:
            xs, tiles, step = (*range(4), *range(12, 16)), ((0, 0), (1, 3)), 2
            field = jnp.concatenate([fe[c, x : x + 4].reshape(64, KZ) for c in range(3) for x in (0, 12)], axis=0)
        lead = f % 2 * 384
        if f == 6:
            product = jnp.dot(field, wz[blk // 2, :, 0:384], preferred_element_type=F32)
        elif f % 2 == 0:
            product = jnp.dot(field, wz[blk // 2], preferred_element_type=F32)
        rows = []
        for c in range(3):
            rows += contract(blk, product, c * len(xs) * step * 8, xs, tiles, step, lead)
        part[f] = jnp.concatenate(rows + [jnp.zeros((4, 128), F32)], axis=0)

    def send_back(i, d):
        copy_of(3, i, d).start()

    each(cross, send_back)
    each(same, send_back)

    def own_moments(pair, carry):
        rows = [[], []]
        for c in range(3):
            product = jnp.dot(fm[c].reshape(CX * CY, KZ), wz[pair], preferred_element_type=F32)
            for i in range(2):
                rows[i] += contract(pair * 2 + i, product, 0, range(CX), own_tiles, CY // 8, i * 384)
        for i in range(2):
            lanes = pl.ds(pl.multiple_of(pair * 256 + i * 128, 128), 128)
            total[:, lanes] = jnp.concatenate(rows[i] + [jnp.zeros((4, 128), F32)], axis=0)
        return carry

    lax.fori_loop(0, BLOCKS // 2, own_moments, 0, unroll=2)

    each(exists, arrived(3))
    high, low = [], []
    for f in range(FOREIGN):
        item = back[f] if f < 6 else corner([back[6 + i] for i in range(4)])
        piece, rest = split(item)
        high.append(piece)
        low.append(rest)
    both = jnp.concatenate([jnp.concatenate(high, axis=1), jnp.concatenate(low, axis=1)], axis=0)
    spread = jnp.dot(both, gm[...], preferred_element_type=F32)
    sums = total[...] + (spread[:16] + spread[16:])
    for blk in range(BLOCKS):
        grad_ref[pl.ds(blk, 12, stride=BLOCKS)] = sums[:12, blk * 128 : blk * 128 + 128]
    own_out.wait()

    def sent(i, d):
        for k in range(4):
            copy_of(k, i, d).wait_send()

    each(exists, sent)


def body(adjoint_velocity, coefficient, record_counts, record_cells, record_offsets):
    nw, nn = lax.axis_size("wide"), lax.axis_size("narrow")
    vmem = pl.BlockSpec(memory_space=pltpu.VMEM)
    hbm = pl.BlockSpec(memory_space=pl.ANY)
    smoothed, grads = pl.pallas_call(
        functools.partial(kernel, nw, nn),
        out_shape=(
            jax.ShapeDtypeStruct((3, CX, CY, NZ), F32),
            jax.ShapeDtypeStruct((12 * BLOCKS, 128), F32),
        ),
        in_specs=[hbm, hbm, hbm, hbm, hbm],
        out_specs=(hbm, vmem),
        scratch_shapes=[
            pltpu.VMEM((3, XU, YB, NZ), F32),
            pltpu.VMEM((XC, YB, NZ), F32),
            pltpu.VMEM((3, XU, YB, NZ), F32),
            pltpu.VMEM((3, XU, YB, NZ), F32),
            pltpu.VMEM((3, XU, YB, NZ), F32),
            pltpu.VMEM((6, XU, YN, NZ), F32),
            pltpu.VMEM((3, CX, CY, KZ), BF16),
            pltpu.VMEM((3, CX, 16, KZ), BF16),
            pltpu.VMEM(((BLOCKS + FOREIGN + 1) // 2, KZ, 768), BF16),
            pltpu.VMEM((BLOCKS + FOREIGN, 3, CY, 128), F32),
            pltpu.VMEM((BLOCKS + FOREIGN, 3, CX, 128), F32),
            pltpu.VMEM((PACKED, SLOTS), BF16),
            pltpu.VMEM((16, SLOTS), BF16),
            pltpu.VMEM((FOREIGN, 8, 128), F32),
            pltpu.VMEM((FOREIGN + 3, 8, 128), F32),
            pltpu.VMEM((FOREIGN, 16, 128), F32),
            pltpu.VMEM((FOREIGN + 3, 16, 128), F32),
            pltpu.VMEM((16, SLOTS), F32),
            pltpu.VMEM((1, 1), jnp.int32),
            pltpu.VMEM((3 * BLOCKS, 128), jnp.int32),
            pltpu.VMEM((3 * BLOCKS, 128), F32),
            pltpu.VMEM((3, CX, CY, NZ), F32),
            pltpu.SemaphoreType.DMA((6,)),
            pltpu.SemaphoreType.DMA((4, 8)),
            pltpu.SemaphoreType.DMA((4, 8)),
        ],
        compiler_params=pltpu.CompilerParams(
            collective_id=0, has_side_effects=True, vmem_limit_bytes=63 << 20
        ),
    )(
        adjoint_velocity,
        coefficient,
        record_counts,
        record_cells.reshape(3 * BLOCKS, 128),
        record_offsets.reshape(3 * BLOCKS, 128),
    )
    return smoothed, grads.reshape(1, 1, 12, SLOTS)


def solution(mesh):
    return jax.shard_map(
        body,
        mesh=mesh,
        in_specs=(
            P(None, "wide", "narrow", None),
            P("wide", "narrow", None),
            P("wide", "narrow"),
            P("wide", "narrow", None, None),
            P("wide", "narrow", None, None),
        ),
        out_specs=(P(None, "wide", "narrow", None), P("wide", "narrow", None, None)),
        check_vma=False,
    )
```

```python
import functools
import math

import jax
import jax.numpy as jnp
from jax import lax
from jax.experimental import pallas as pl
from jax.experimental.pallas import tpu as pltpu
from jax.sharding import PartitionSpec as P

MESH = pl.DeviceIdType.MESH
F32 = jnp.float32
BF16 = jnp.bfloat16

RADIUS = 4
CX, CY, NZ = 16, 32, 128
SLOTS = 1024
BLOCKS = SLOTS // 128
HU = 3
HC = 4
XU = CX + 2 * HU
XC = CX + 2 * HC
YA = 8
YN = CY + 8
Y0 = YA + 4
YB = YN + 16
TILES = YN // 8
KZ = 3 * NZ
FOREIGN = 7
PACKED = FOREIGN * 128
CLASSES = (
    ((-1, 0), 0, 256),
    ((1, 0), 256, 256),
    ((0, -1), 512, 128),
    ((0, 1), 640, 128),
    ((-1, -1), 768, 32),
    ((-1, 1), 800, 32),
    ((1, -1), 832, 32),
    ((1, 1), 864, 32),
)
CORNERS = ((-1, -1), (-1, 1), (1, -1), (1, 1))

WIDTH = 1.25
RELAX = 0.8

DIRS = [(dx, dy) for dx in (-1, 0, 1) for dy in (-1, 0, 1) if (dx, dy) != (0, 0)]


def profile(distance):
    width_sq = WIDTH * WIDTH
    base = jnp.exp(-distance * distance / (2.0 * width_sq)) / (WIDTH * math.sqrt(2.0 * math.pi))
    first = -distance / width_sq * base
    second = (distance * distance / width_sq - 1.0) / width_sq * base
    return (base, first, second)


def weights(places, centre, offset):
    distance = places - centre
    inside = jnp.abs(distance) <= RADIUS
    return [jnp.where(inside, item, 0.0) for item in profile(distance + 0.5 - offset)]


def split(value):
    high = value.astype(BF16)
    return high, (value - high.astype(F32)).astype(BF16)


def blocks_of(d, landing):
    if d[0] and d[1]:
        return pl.ds(6 + (CORNERS.index(d) if landing else 0), 1)
    return {(-1, 0): pl.ds(0, 2), (1, 0): pl.ds(2, 2), (0, -1): pl.ds(4, 1), (0, 1): pl.ds(5, 1)}[d]


def along(d, low, own, high):
    return (low, own, high)[d + 1]


def kernel(
    nw, nn, u_ref, k_ref, counts, cells, offsets, out, grad_ref,
    ub, cb, w1, wa, wb, ck, fm, fe, wz, wy, wx, gm, dm, mine, theirs, part, back, total, count_ref, cell_ref, off_ref, out_ref,
    own_sem, send_sem, recv_sem,
):
    a, b = lax.axis_index("wide"), lax.axis_index("narrow")
    half = nn // 2

    def exists(d):
        return (a + d[0] >= 0) & (a + d[0] < nw) & (b + d[1] >= 0) & (b + d[1] < nn)

    def same(d):
        if d[1] == 0:
            return exists(d)
        return exists(d) & ((b < half) == (b + d[1] < half))

    def cross(d):
        if d[1] == 0:
            return None
        return exists(d) & ((b < half) != (b + d[1] < half))

    def each(test, action):
        for i, d in enumerate(DIRS):
            ok = test(d)
            if ok is not None:
                pl.when(ok)(functools.partial(action, i, d))

    def number(test):
        return sum(jnp.where(test(d), 1, 0) for d in DIRS if test(d) is not None)

    def copy_of(k, i, d):
        x, y = d
        to = (a + x, b + y)

        def remote(k, src, dst):
            return pltpu.make_async_remote_copy(
                src_ref=src, dst_ref=dst, send_sem=send_sem.at[k, i], recv_sem=recv_sem.at[k, i],
                device_id=to, device_id_type=MESH,
            )

        def parts(n, lo_x, lo_y):
            src = (
                along(x, pl.ds(lo_x, n), pl.ds(lo_x, CX), pl.ds(lo_x + CX - n, n)),
                along(y, pl.ds(lo_y, n), pl.ds(lo_y, CY), pl.ds(lo_y + CY - n, n)),
            )
            dst = (
                along(x, pl.ds(lo_x + CX, n), pl.ds(lo_x, CX), pl.ds(lo_x - n, n)),
                along(y, pl.ds(lo_y + CY, n), pl.ds(lo_y, CY), pl.ds(lo_y - n, n)),
            )
            return src, dst

        if k == 0:
            src, dst = parts(HC, HC, Y0)
            return remote(k, cb.at[src], cb.at[dst])
        if k == 1:
            src, dst = parts(HU, HU, Y0)
            return remote(k, ub.at[:, src[0], src[1]], ub.at[:, dst[0], dst[1]])
        if k == 2:
            return remote(k, mine.at[blocks_of(d, False)], theirs.at[blocks_of(d, True)])
        came = (-x, -y)
        return remote(k, part.at[blocks_of(came, False)], back.at[blocks_of(came, True)])

    barrier = pltpu.get_barrier_semaphore()

    def signal(i, d):
        pl.semaphore_signal(barrier, inc=1, device_id=(a + d[0], b + d[1]), device_id_type=MESH)

    def send(i, d):
        for k in range(3):
            copy_of(k, i, d).start()

    each(exists, signal)
    own_k = pltpu.make_async_copy(k_ref, cb.at[pl.ds(HC, CX), pl.ds(Y0, CY)], own_sem.at[0])
    own_u = pltpu.make_async_copy(u_ref, ub.at[:, pl.ds(HU, CX), pl.ds(Y0, CY)], own_sem.at[1])
    own_cells = pltpu.make_async_copy(cells, cell_ref, own_sem.at[2])
    own_offsets = pltpu.make_async_copy(offsets, off_ref, own_sem.at[3])
    own_count = pltpu.make_async_copy(counts, count_ref, own_sem.at[5])
    for copy in (own_count, own_cells, own_offsets, own_k, own_u):
        copy.start()

    @pl.when(a == 0)
    def _():
        ub[:, 0:HU] = jnp.zeros((3, HU, YB, NZ), F32)
        cb[0:HC] = jnp.zeros((HC, YB, NZ), F32)

    @pl.when(a == nw - 1)
    def _():
        ub[:, HU + CX :] = jnp.zeros((3, HU, YB, NZ), F32)
        cb[HC + CX :] = jnp.zeros((HC, YB, NZ), F32)

    @pl.when(b == 0)
    def _():
        ub[:, :, Y0 - 4 : Y0] = jnp.zeros((3, XU, 4, NZ), F32)
        cb[:, Y0 - 4 : Y0] = jnp.zeros((XC, 4, NZ), F32)

    @pl.when(b == nn - 1)
    def _():
        ub[:, :, Y0 + CY : Y0 + CY + 4] = jnp.zeros((3, XU, 4, NZ), F32)
        cb[:, Y0 + CY : Y0 + CY + 4] = jnp.zeros((XC, 4, NZ), F32)

    for d in DIRS:

        @pl.when(jnp.logical_not(exists(d)))
        def _():
            at, came = blocks_of(d, True), blocks_of((-d[0], -d[1]), True)
            back[at] = jnp.zeros((at.size, 16, 128), F32)
            theirs[came] = jnp.zeros((came.size, 8, 128), F32)

    lane1 = lax.broadcasted_iota(jnp.int32, (1, 128), 1)
    before = lax.broadcasted_iota(jnp.int32, (128, 128), 0) < lax.broadcasted_iota(jnp.int32, (128, 128), 1)
    before = jnp.where(before, 1.0, 0.0).astype(BF16)
    starts = jnp.concatenate([jnp.full((1, 128), first, F32) for _, first, _ in CLASSES], axis=0)

    def record(blk):
        centre = [cell_ref[pl.ds(d * BLOCKS + blk, 1)].astype(F32) for d in range(3)]
        offset = [off_ref[pl.ds(d * BLOCKS + blk, 1)] for d in range(3)]
        live = jnp.where(lane1 + blk * 128 < count_ref[...], 1.0, 0.0)
        return centre, offset, live

    def pack(blk, seen):
        lanes = pl.ds(pl.multiple_of(blk * 128, 128), 128)
        centre, offset, live = record(blk)
        reach = {
            (0, -1): centre[0] < RADIUS, (0, 1): centre[0] >= CX - RADIUS,
            (1, -1): centre[1] < RADIUS, (1, 1): centre[1] >= CY - RADIUS,
        }
        member = []
        for d, _, _ in CLASSES:
            one = jnp.ones((1, 128), F32)
            for axis in range(2):
                if d[axis]:
                    one = jnp.where(reach[axis, d[axis]], one, 0.0)
            member.append(one)
        member = jnp.concatenate(member, axis=0)
        place = jnp.dot(member.astype(BF16), before, preferred_element_type=F32) + seen + starts
        place = jnp.where(member > 0.0, place, -1.0)
        for i, (_, first, size) in enumerate(CLASSES):
            rows = lax.broadcasted_iota(jnp.int32, (size, 128), 0).astype(F32) + float(first)
            gm[first : first + size, lanes] = jnp.where(rows == place[i : i + 1], 1.0, 0.0).astype(BF16)
        pieces = list(centre)
        rest = offset
        for _ in range(3):
            high = [item.astype(BF16).astype(F32) for item in rest]
            rest = [item - piece for item, piece in zip(rest, high)]
            pieces += high
        pieces += [live] + [jnp.zeros((1, 128), F32)] * 3
        dm[:, lanes] = jnp.concatenate(pieces, axis=0).astype(BF16)
        return seen + jnp.sum(member, axis=1, keepdims=True)

    own_count.wait()
    own_cells.wait()
    own_offsets.wait()
    lax.fori_loop(0, BLOCKS, pack, jnp.zeros((8, 128), F32))
    packed = lax.dot_general(dm[...], gm[...], (((1,), (1,)), ((), ())), preferred_element_type=F32)
    for f in range(FOREIGN):
        item = packed[:, f * 128 : f * 128 + 128]
        offset = item[3:6] + (item[6:9] + item[9:12])
        mine[f] = jnp.concatenate([item[0:3], offset, item[12:14]], axis=0)

    own_k.wait()
    own_u.wait()
    pl.semaphore_wait(barrier, number(exists))
    each(cross, send)
    each(same, send)

    def prepare(blk, centre, offset, live):
        def at(i):
            start = blk % 2 * 384 + i * 128
            return pl.ds(start if isinstance(blk, int) else pl.multiple_of(start, 128), 128)

        rows = lax.broadcasted_iota(jnp.int32, (NZ, 128), 0).astype(F32)
        for i, item in enumerate(weights(rows, centre[2], offset[2])):
            high, low = split(item)
            wz[blk // 2, 0:128, at(i)] = high
            wz[blk // 2, 128:256, at(i)] = high
            wz[blk // 2, 256:384, at(i)] = low
        rows = lax.broadcasted_iota(jnp.int32, (CY, 128), 0).astype(F32)
        for i, item in enumerate(weights(rows, centre[1], offset[1])):
            wy[blk, i] = item
        for i, item in enumerate(weights(rows[:CX], centre[0], offset[0])):
            wx[blk, i] = item * live

    def prepare_own(blk, carry):
        prepare(blk, *record(blk))
        return carry

    lax.fori_loop(0, BLOCKS, prepare_own, 0)

    def arrived(k):
        def action(i, d):
            j = DIRS.index((-d[0], -d[1]))
            copy_of(k, j, DIRS[j]).wait_recv()

        return action

    def corner(values):
        result = values[3]
        for i in (2, 1, 0):
            result = jnp.where(lane1 < 32 * (i + 1), values[i], result)
        return result

    each(exists, arrived(2))
    for f in range(FOREIGN):
        if f < 6:
            item = theirs[f]
            dx, dy = ((-1, 0), (-1, 0), (1, 0), (1, 0), (0, -1), (0, 1))[f]
            shift = -float(dx * CX), -float(dy * CY)
        else:
            item = corner([theirs[6 + i] for i in range(4)])
            shift = [corner([jnp.full((1, 128), -float(d[axis] * n), F32) for d in CORNERS]) for axis, n in ((0, CX), (1, CY))]
        centre = [item[0:1] + shift[0], item[1:2] + shift[1], item[2:3]]
        prepare(BLOCKS + f, centre, [item[3:4], item[4:5], item[5:6]], item[6:7])


    each(exists, arrived(0))
    each(exists, arrived(1))

    lane = lax.broadcasted_iota(jnp.int32, (8, NZ), 1)
    last_z, first_z = lane == NZ - 1, lane == 0
    y_at = lax.broadcasted_iota(jnp.int32, (8, NZ), 0) + (b * CY - 4)

    def face_coefficients(x, carry):
        x_at = a * CX - HU + x
        x_in = (x_at >= 0) & (x_at < nw * CX)
        for t in range(TILES):
            r = YA + 8 * t
            mid = cb[x + 1, r : r + 8]
            beside = [
                cb[x + 2, r : r + 8],
                cb[x, r : r + 8],
                cb[x + 1, r + 1 : r + 9],
                cb[x + 1, r - 1 : r + 7],
                jnp.where(last_z, 0.0, pltpu.roll(mid, NZ - 1, 1)),
                jnp.where(first_z, 0.0, pltpu.roll(mid, 1, 1)),
            ]
            faces = [0.5 * (mid + item) for item in beside]
            total = 1.0 + sum(faces)
            y = y_at + 8 * t
            scale = jnp.where((y >= 0) & (y < nn * CY) & x_in, RELAX / total, 0.0)
            faces[4] = jnp.where(last_z, 0.0, faces[4])
            faces[5] = jnp.where(first_z, 0.0, faces[5])
            for i, face in enumerate(faces):
                ck[i, x, 8 * t : 8 * t + 8] = scale * face
            for c in range(3):
                w1[c, x, r : r + 8] = scale * ub[c, x, r : r + 8]
        return carry

    lax.fori_loop(0, XU, face_coefficients, 0, unroll=11)

    def relaxed(src, x):
        values = [[], [], []]
        for t in range(TILES):
            r = YA + 8 * t
            k = [ck[i, x, 8 * t : 8 * t + 8] for i in range(6)]
            for c in range(3):
                mid = src[c, x, r : r + 8]
                total = (1.0 - RELAX) * mid + w1[c, x, r : r + 8]
                ends = k[4] * pltpu.roll(mid, NZ - 1, 1) + k[5] * pltpu.roll(mid, 1, 1)
                sides = k[2] * src[c, x, r + 1 : r + 9] + k[3] * src[c, x, r - 1 : r + 7]
                total += k[0] * src[c, x + 1, r : r + 8] + k[1] * src[c, x - 1, r : r + 8]
                values[c].append(total + sides + ends)
        return values

    def sweep(src, dst):
        def step(x, carry):
            values = relaxed(src, x)
            for c in range(3):
                for t in range(TILES):
                    dst[c, x, YA + 8 * t : YA + 8 * t + 8] = values[c][t]
            return carry

        return step

    lax.fori_loop(1, XU - 1, sweep(w1, wa), 0, unroll=10)
    lax.fori_loop(2, XU - 2, sweep(wa, wb), 0, unroll=9)

    def store_split(ref, index, value):
        high, low = split(value)
        ref[(*index, slice(0, 128))] = high
        ref[(*index, slice(128, 256))] = low
        ref[(*index, slice(256, 384))] = high

    def last(x, carry):
        values = relaxed(wb, x)
        for c in range(3):
            out_ref[c, x - HU] = jnp.concatenate(values[c], axis=0)[4 : 4 + CY]
        return carry

    lax.fori_loop(HU, HU + CX, last, 0, unroll=8)

    own_out = pltpu.make_async_copy(out_ref, out, own_sem.at[4])
    own_out.start()

    def split_own(x, carry):
        for c in range(3):
            field = out_ref[c, x]
            store_split(fm, (c, x, slice(None)), field)
            store_split(fe, (c, x, slice(None)), jnp.concatenate([field[:8], field[CY - 8 :]], axis=0))
        return carry

    lax.fori_loop(0, CX, split_own, 0, unroll=8)

    def contract(blk, product, row, xs, tiles, step, lead):
        sums = [jnp.zeros((8, 128), F32) for _ in range(4)]
        for n, x in enumerate(xs):
            along0 = along1 = slope = bend = None
            for at, t in tiles:
                r = row + (n * step + at) * 8
                t0, t1, t2 = [product[r : r + 8, lead + i * 128 : lead + i * 128 + 128] for i in range(3)]
                g0, g1, g2 = [wy[blk, i, t * 8 : t * 8 + 8] for i in range(3)]
                terms = t0 * g0, t1 * g0, t0 * g1, t0 * g2 + t2 * g0
                if along0 is None:
                    along0, along1, slope, bend = terms
                else:
                    along0, along1, slope, bend = [p + q for p, q in zip((along0, along1, slope, bend), terms)]
            x0, x1, x2 = [wx[blk, i, x : x + 1] for i in range(3)]
            sums[0] += along0 * x1
            sums[1] += slope * x0
            sums[2] += along1 * x0
            sums[3] += along0 * x2 + bend * x0
        return [jnp.sum(item, axis=0, keepdims=True) for item in sums]

    own_tiles = tuple((t, t) for t in range(CY // 8))
    def send_back(turned, i, d):
        if bool(d[1]) == turned:
            copy_of(3, i, d).start()

    for f in (4, 5, 6, 0, 1, 2, 3):
        blk = BLOCKS + f
        if f < 4:
            xs, tiles, step = range(12, 16) if f < 2 else range(4), own_tiles, CY // 8
            field = fm[:, xs[0] : xs[0] + 4].reshape(3 * 4 * CY, KZ)
        elif f < 6:
            xs, tiles, step = range(CX), (((1, 3),), ((0, 0),))[f - 4], 2
            field = fe[...].reshape(3 * CX * 16, KZ)
        else:
            xs, tiles, step = (*range(4), *range(12, 16)), ((0, 0), (1, 3)), 2
            field = jnp.concatenate([fe[c, x : x + 4].reshape(64, KZ) for c in range(3) for x in (0, 12)], axis=0)
        lead = f % 2 * 384
        if f == 6:
            product = jnp.dot(field, wz[blk // 2, :, 0:384], preferred_element_type=F32)
        elif f % 2 == 0:
            product = jnp.dot(field, wz[blk // 2], preferred_element_type=F32)
        rows = []
        for c in range(3):
            rows += contract(blk, product, c * len(xs) * step * 8, xs, tiles, step, lead)
        part[f] = jnp.concatenate(rows + [jnp.zeros((4, 128), F32)], axis=0)
        if f == 6:
            each(cross, functools.partial(send_back, True))
            each(same, functools.partial(send_back, True))
    each(same, functools.partial(send_back, False))


    def own_moments(pair, carry):
        rows = [[], []]
        for c in range(3):
            product = jnp.dot(fm[c].reshape(CX * CY, KZ), wz[pair], preferred_element_type=F32)
            for i in range(2):
                rows[i] += contract(pair * 2 + i, product, 0, range(CX), own_tiles, CY // 8, i * 384)
        for i in range(2):
            lanes = pl.ds(pl.multiple_of(pair * 256 + i * 128, 128), 128)
            total[:, lanes] = jnp.concatenate(rows[i] + [jnp.zeros((4, 128), F32)], axis=0)
        return carry

    lax.fori_loop(0, BLOCKS // 2, own_moments, 0, unroll=2)

    each(exists, arrived(3))
    high, low = [], []
    for f in range(FOREIGN):
        item = back[f] if f < 6 else corner([back[6 + i] for i in range(4)])
        piece, rest = split(item)
        high.append(piece)
        low.append(rest)
    both = jnp.concatenate([jnp.concatenate(high, axis=1), jnp.concatenate(low, axis=1)], axis=0)
    spread = jnp.dot(both, gm[...], preferred_element_type=F32)
    sums = total[...] + (spread[:16] + spread[16:])
    for blk in range(BLOCKS):
        grad_ref[pl.ds(blk, 12, stride=BLOCKS)] = sums[:12, blk * 128 : blk * 128 + 128]
    own_out.wait()

    def sent(i, d):
        for k in range(4):
            copy_of(k, i, d).wait_send()

    each(exists, sent)


def body(adjoint_velocity, coefficient, record_counts, record_cells, record_offsets):
    nw, nn = lax.axis_size("wide"), lax.axis_size("narrow")
    vmem = pl.BlockSpec(memory_space=pltpu.VMEM)
    hbm = pl.BlockSpec(memory_space=pl.ANY)
    smoothed, grads = pl.pallas_call(
        functools.partial(kernel, nw, nn),
        out_shape=(
            jax.ShapeDtypeStruct((3, CX, CY, NZ), F32),
            jax.ShapeDtypeStruct((12 * BLOCKS, 128), F32),
        ),
        in_specs=[hbm, hbm, hbm, hbm, hbm],
        out_specs=(hbm, vmem),
        scratch_shapes=[
            pltpu.VMEM((3, XU, YB, NZ), F32),
            pltpu.VMEM((XC, YB, NZ), F32),
            pltpu.VMEM((3, XU, YB, NZ), F32),
            pltpu.VMEM((3, XU, YB, NZ), F32),
            pltpu.VMEM((3, XU, YB, NZ), F32),
            pltpu.VMEM((6, XU, YN, NZ), F32),
            pltpu.VMEM((3, CX, CY, KZ), BF16),
            pltpu.VMEM((3, CX, 16, KZ), BF16),
            pltpu.VMEM(((BLOCKS + FOREIGN + 1) // 2, KZ, 768), BF16),
            pltpu.VMEM((BLOCKS + FOREIGN, 3, CY, 128), F32),
            pltpu.VMEM((BLOCKS + FOREIGN, 3, CX, 128), F32),
            pltpu.VMEM((PACKED, SLOTS), BF16),
            pltpu.VMEM((16, SLOTS), BF16),
            pltpu.VMEM((FOREIGN, 8, 128), F32),
            pltpu.VMEM((FOREIGN + 3, 8, 128), F32),
            pltpu.VMEM((FOREIGN, 16, 128), F32),
            pltpu.VMEM((FOREIGN + 3, 16, 128), F32),
            pltpu.VMEM((16, SLOTS), F32),
            pltpu.VMEM((1, 1), jnp.int32),
            pltpu.VMEM((3 * BLOCKS, 128), jnp.int32),
            pltpu.VMEM((3 * BLOCKS, 128), F32),
            pltpu.VMEM((3, CX, CY, NZ), F32),
            pltpu.SemaphoreType.DMA((6,)),
            pltpu.SemaphoreType.DMA((4, 8)),
            pltpu.SemaphoreType.DMA((4, 8)),
        ],
        compiler_params=pltpu.CompilerParams(
            collective_id=0, has_side_effects=True, vmem_limit_bytes=63 << 20
        ),
    )(
        adjoint_velocity,
        coefficient,
        record_counts,
        record_cells.reshape(3 * BLOCKS, 128),
        record_offsets.reshape(3 * BLOCKS, 128),
    )
    return smoothed, grads.reshape(1, 1, 12, SLOTS)


def solution(mesh):
    return jax.shard_map(
        body,
        mesh=mesh,
        in_specs=(
            P(None, "wide", "narrow", None),
            P("wide", "narrow", None),
            P("wide", "narrow"),
            P("wide", "narrow", None, None),
            P("wide", "narrow", None, None),
        ),
        out_specs=(P(None, "wide", "narrow", None), P("wide", "narrow", None, None)),
        check_vma=False,
    )
```
